128 devices in a mesh: seq: 32 (over x_lo, y, z), ch: 4 (over x_hi, core).
Axes of the slice: x: 4 (x_hi: 2, x_lo: 2; x = x_hi * 2 + x_lo), y: 4, z: 4, core: 2. Of those that a mesh axis runs over, the one named last changes fastest.
Arguments:
- projected: bfloat16 [3, 16384, 8192], P(None, 'seq', 'ch'), may hold values from -6 to 6
- short_filters: float32 [3, 3, 8192], P(None, None, 'ch'), may hold values from -3.5 to 3.5
- long_filter: float32 [128, 8192], P(None, 'ch'), may hold values from -0.5 to 0.5
- skip_gain: float32 [8192], P('ch'), may hold values from -4 to 4
- cotangent: bfloat16 [16384, 8192], P(('seq', 'ch')), may hold values from -6 to 6
Outputs:
- grad_input: bfloat16 [3, 16384, 8192], P(None, 'seq', 'ch')
- grad_long: float32 [128, 8192], P(None, 'ch')
- grad_skip: float32 [8192], P('ch')
- grad_short: float32 [3, 3, 8192], P(None, None, 'ch')
The draws below stay inside these ranges and needn't reach their ends.
All inputs are finite; a program needn't handle non-finite values.
Results may differ from the reference program's by a relative error of at most 0.0057.
Values may be sent and summed in bfloat16 or wider, within the bound.
A program may use at most 128 MiB of HBM per device.

```python
import math
import jax
import jax.numpy as jnp
from jax import lax

D = 8192
TAPS = 128
SHORT = 3
TOKENS = 16384


def levels(rng, extent, pieces, smallest, high):
    def one(axis_at, parts):
        steps = jax.random.uniform(jax.random.fold_in(jax.random.fold_in(rng, 6), axis_at), (parts,), jnp.float32, smallest / len(pieces), high / len(pieces))
        return jnp.repeat(jnp.exp(steps), extent[axis_at] // parts).reshape((-1,) + (1,) * (len(extent) - axis_at - 1))

    loudness = one(*pieces[0])
    for cut in pieces[1:]:
        loudness = loudness * one(*cut)
    return loudness


def centred(key, dims, scale, most, shards=(), kind=jnp.bfloat16):
    level = levels(key, dims, shards, -0.22, 0.18) if shards else 1.0
    array = jax.random.normal(key, dims, jnp.float32) * scale * level
    return jnp.minimum(jnp.maximum(array, -most), most).astype(kind)


def setup_inputs(seed: int = 0) -> dict:
    keys = jax.random.split(jax.random.key(seed), 6)
    return {
        "projected": centred(keys[0], (3, TOKENS, D), 1.0, 6.0, ((1, 32), (2, 4))),
        "short_filters": centred(keys[1], (3, SHORT, D), SHORT ** -0.5, 3.5, ((2, 4),), jnp.float32),
        "long_filter": centred(keys[2], (TAPS, D), TAPS ** -0.5, 0.5, ((1, 4),), jnp.float32),
        "skip_gain": centred(keys[3], (D,), 1.0, 4.0, ((0, 4),), jnp.float32),
        "cotangent": centred(keys[4], (TOKENS, D), 1.0, 6.0, ((0, 128),)),
    }


def delayed(values, offset):
    if offset == 0:
        return values
    zeros = jnp.zeros_like(values[..., :offset, :])
    return jnp.concatenate([zeros, values[..., :-offset, :]], axis=-2)


def advanced(values, offset):
    if offset == 0:
        return values
    zeros = jnp.zeros_like(values[..., :offset, :])
    return jnp.concatenate([values[..., offset:, :], zeros], axis=-2)


def causal(signal, filters):
    length = signal.shape[0]
    total = length + filters.shape[0]
    product = jnp.fft.rfft(signal, n=total, axis=0) * jnp.fft.rfft(filters, n=total, axis=0)
    return jnp.fft.irfft(product, n=total, axis=0)[:length]


def lagged_products(later, earlier, count):
    total = later.shape[0] + count
    product = jnp.fft.rfft(later, n=total, axis=0) * jnp.conj(jnp.fft.rfft(earlier, n=total, axis=0))
    return jnp.fft.irfft(product, n=total, axis=0)[:count]


def channel_block(inputs):
    projected, short_filters, long_filter, skip_gain, cotangent = inputs
    inputs_f = projected.astype(jnp.float32)
    streams = short_filters[:, 0][:, None, :] * inputs_f
    for offset in range(1, SHORT):
        streams = streams + short_filters[:, offset][:, None, :] * delayed(inputs_f, offset)
    query_rows, key_rows, value_rows = streams[0], streams[1], streams[2]
    gated = (key_rows * value_rows).astype(jnp.bfloat16)
    gated = lax.optimization_barrier(gated)
    gated_f = gated.astype(jnp.float32)
    long_mixed = causal(gated_f, long_filter) + skip_gain * gated_f
    upstream = cotangent.astype(jnp.float32)
    d_query = (upstream * long_mixed).astype(jnp.bfloat16)
    d_mixed = (upstream * query_rows).astype(jnp.bfloat16)
    d_mixed = lax.optimization_barrier(d_mixed)
    d_mixed_f = d_mixed.astype(jnp.float32)
    d_gated = causal(d_mixed_f[::-1], long_filter)[::-1] + skip_gain * d_mixed_f
    d_key = (d_gated * value_rows).astype(jnp.bfloat16)
    d_value = (d_gated * key_rows).astype(jnp.bfloat16)
    stream_grads = lax.optimization_barrier(jnp.stack([d_query, d_key, d_value]))
    grads_f = stream_grads.astype(jnp.float32)
    factor = float(TOKENS) ** -0.5
    grad_long = lagged_products(d_mixed_f, gated_f, TAPS) * factor
    grad_skip = jnp.sum(d_mixed_f * gated_f, axis=0) * factor
    grad_short = jnp.stack([jnp.sum(grads_f * delayed(inputs_f, offset), axis=1) for offset in range(SHORT)], axis=1) * factor
    grad_input = short_filters[:, 0][:, None, :] * grads_f
    for offset in range(1, SHORT):
        grad_input = grad_input + short_filters[:, offset][:, None, :] * advanced(grads_f, offset)
    return grad_input.astype(jnp.bfloat16), grad_long, grad_skip, grad_short


def reference(projected, short_filters, long_filter, skip_gain, cotangent):
    width = math.gcd(D, 1024)
    blocks = D // width
    inputs = (
        projected.reshape(3, TOKENS, blocks, width).transpose(2, 0, 1, 3),
        short_filters.reshape(3, SHORT, blocks, width).transpose(2, 0, 1, 3),
        long_filter.reshape(TAPS, blocks, width).transpose(1, 0, 2),
        skip_gain.reshape(blocks, width),
        cotangent.reshape(TOKENS, blocks, width).transpose(1, 0, 2),
    )
    grad_input, grad_long, grad_skip, grad_short = lax.map(channel_block, inputs)
    grad_input = grad_input.transpose(1, 2, 0, 3).reshape(3, TOKENS, D)
    grad_long = grad_long.transpose(1, 0, 2).reshape(TAPS, D)
    grad_skip = grad_skip.reshape(D)
    grad_short = grad_short.transpose(1, 2, 0, 3).reshape(3, SHORT, D)
    return grad_input, grad_long, grad_skip, grad_short
```

```python
import jax
import jax.numpy as jnp
from jax import lax
from jax.experimental import pallas as pl
from jax.experimental.pallas import tpu as pltpu
from jax.sharding import PartitionSpec as P

TAPS = 128
SHORT = 3


def passed_along(value, axis, steps):
    count = lax.axis_size(axis)
    initial, last = (max(0, -steps), min(count, count - steps))
    return lax.ppermute(value, axis, [(source, source + steps) for source in range(initial, last)])


def correlate(extended, kernel, accuracy):
    channels = extended.shape[1]
    result = lax.conv_general_dilated(
        extended[None],
        kernel[:, None, :],
        (1,),
        "VALID",
        dimension_numbers=("NWC", "WIO", "NWC"),
        feature_group_count=channels,
        precision=accuracy,
        preferred_element_type=jnp.float32,
    )
    return result[0]


def short_forward(extended, short_filters, count):
    short_lag = SHORT - 1
    streams = jnp.zeros((3, count, extended.shape[2]), jnp.float32)
    for offset in range(SHORT):
        window = extended[:, short_lag - offset : short_lag - offset + count, :].astype(jnp.float32)
        streams = streams + short_filters[:, offset][:, None, :] * window
    return streams


PEERS = 32
PIECE = 1152
MESH = pl.DeviceIdType.MESH


def all_reduce_kernel(long_ref, rest_ref, long_out, rest_out, parts, landed, total, gathered, sems):
    me = lax.axis_index("seq")
    barrier = pltpu.get_barrier_semaphore()

    @pl.loop(1, PEERS)
    def _(k):
        pl.semaphore_signal(barrier, inc=1, device_id={"seq": lax.rem(me + k, PEERS)}, device_id_type=MESH)

    for p in range(PEERS):
        row, half = p // 2, p % 2
        parts[p, :, :1024] = long_ref[8 * row : 8 * row + 8, 1024 * half : 1024 * half + 1024]
        row, tile = p // 16, p % 16
        parts[p, :, 1024:] = rest_ref[8 * row : 8 * row + 8, 128 * tile : 128 * tile + 128]
    pl.semaphore_wait(barrier, PEERS - 1)

    @pl.loop(1, PEERS)
    def _(k):
        peer = lax.rem(me + k, PEERS)
        pltpu.make_async_remote_copy(
            src_ref=parts.at[peer],
            dst_ref=landed.at[k - 1],
            send_sem=sems.at[0],
            recv_sem=sems.at[1],
            device_id={"seq": peer},
            device_id_type=MESH,
        ).start()

    pltpu.make_async_copy(landed, landed, sems.at[1]).wait()
    acc = parts[me]
    for k in range(PEERS - 1):
        acc = acc + landed[k]
    total[...] = acc
    gathered[me] = acc

    @pl.loop(1, PEERS)
    def _(k):
        peer = lax.rem(me + k, PEERS)
        pltpu.make_async_remote_copy(
            src_ref=total,
            dst_ref=gathered.at[me],
            send_sem=sems.at[2],
            recv_sem=sems.at[3],
            device_id={"seq": peer},
            device_id_type=MESH,
        ).start()

    pltpu.make_async_copy(landed, landed, sems.at[0]).wait()
    pltpu.make_async_copy(landed, landed, sems.at[3]).wait()
    pltpu.make_async_copy(landed, landed, sems.at[2]).wait()
    for p in range(PEERS):
        row, half = p // 2, p % 2
        long_out[8 * row : 8 * row + 8, 1024 * half : 1024 * half + 1024] = gathered[p, :, :1024]
        row, tile = p // 16, p % 16
        rest_out[8 * row : 8 * row + 8, 128 * tile : 128 * tile + 128] = gathered[p, :, 1024:]


def all_reduce(long_partial, rest):
    return pl.pallas_call(
        all_reduce_kernel,
        out_shape=(
            jax.ShapeDtypeStruct(long_partial.shape, jnp.float32),
            jax.ShapeDtypeStruct(rest.shape, jnp.float32),
        ),
        in_specs=[pl.BlockSpec(memory_space=pltpu.VMEM)] * 2,
        out_specs=[pl.BlockSpec(memory_space=pltpu.VMEM)] * 2,
        scratch_shapes=[
            pltpu.VMEM((PEERS, 8, PIECE), jnp.float32),
            pltpu.VMEM((PEERS - 1, 8, PIECE), jnp.float32),
            pltpu.VMEM((8, PIECE), jnp.float32),
            pltpu.VMEM((PEERS, 8, PIECE), jnp.float32),
            pltpu.SemaphoreType.DMA((4,)),
        ],
        compiler_params=pltpu.CompilerParams(collective_id=0, has_side_effects=True, vmem_limit_bytes=32 << 20),
    )(long_partial, rest)


def per_device(projected, short_filters, long_filter, skip_gain, cotangent):
    length = projected.shape[1]
    short_lag = SHORT - 1
    long_reach = TAPS - 1
    highest = lax.Precision.HIGHEST
    before = passed_along(projected[:, length - short_lag :, :], "seq", 1)
    own_input = jnp.concatenate([before, projected], axis=1)
    streams = short_forward(own_input, short_filters, length)
    gated = (streams[1] * streams[2]).astype(jnp.bfloat16)
    gated = lax.optimization_barrier(gated)
    earlier = passed_along(gated[length - long_reach :], "seq", 1)
    gated_ext = jnp.concatenate([earlier, gated], axis=0)
    query_rows, key_rows, value_rows = (streams[0], streams[1], streams[2])
    gated_f = gated_ext.astype(jnp.float32)
    own_gated = gated_f[long_reach:]
    long_mixed = correlate(gated_f, long_filter[::-1], highest) + skip_gain * own_gated
    local_grad = lax.all_to_all(cotangent, "ch", split_axis=1, concat_axis=0, tiled=True)
    upstream = local_grad.astype(jnp.float32)
    d_query = (upstream * long_mixed).astype(jnp.bfloat16)
    d_mixed = (upstream * query_rows).astype(jnp.bfloat16)
    d_mixed = lax.optimization_barrier(d_mixed)
    d_mixed_f = d_mixed.astype(jnp.float32)
    following = passed_along(d_mixed[:long_reach], "seq", -1)
    mixed_ext = jnp.concatenate([d_mixed, following], axis=0).astype(jnp.float32)
    d_gated = correlate(mixed_ext, long_filter, highest) + skip_gain * d_mixed_f
    d_key = (d_gated * value_rows).astype(jnp.bfloat16)
    d_value = (d_gated * key_rows).astype(jnp.bfloat16)
    stream_grads = lax.optimization_barrier(jnp.stack([d_query, d_key, d_value]))
    next_terms = passed_along(stream_grads[:, :short_lag], "seq", -1)
    terms_ext = jnp.concatenate([stream_grads, next_terms], axis=1)
    grad_input = jnp.zeros((3, length, d_mixed.shape[1]), jnp.float32)
    for offset in range(SHORT):
        grad_input = grad_input + short_filters[:, offset][:, None, :] * terms_ext[
            :, offset : offset + length, :
        ].astype(jnp.float32)
    long_partial = correlate(gated_ext, d_mixed, None)[::-1]
    skip_partial = jnp.sum(d_mixed_f * own_gated, axis=0)
    short_partial = jnp.stack(
        [
            jnp.einsum(
                "itc,itc->ic",
                stream_grads,
                own_input[:, short_lag - offset : short_lag - offset + length, :],
                preferred_element_type=jnp.float32,
            )
            for offset in range(SHORT)
        ],
        axis=1,
    )
    rest = jnp.concatenate([skip_partial[None], short_partial.reshape(9, -1), jnp.zeros((6, skip_partial.shape[0]), jnp.float32)])
    long_sum, rest_sum = all_reduce(long_partial.reshape(TAPS, -1), rest)
    reduced = (long_sum, rest_sum[0], rest_sum[1:10].reshape(3, SHORT, -1))
    factor = float(length * lax.axis_size("seq")) ** (-0.5)
    return (
        grad_input.astype(jnp.bfloat16),
        reduced[0] * factor,
        reduced[1] * factor,
        reduced[2] * factor,
    )


def solution(mesh):
    placed = (
        P(None, "seq", "ch"),
        P(None, None, "ch"),
        P(None, "ch"),
        P("ch"),
        P(("seq", "ch"), None),
    )
    return jax.shard_map(
        per_device,
        mesh=mesh,
        in_specs=placed,
        out_specs=(P(None, "seq", "ch"), P(None, "ch"), P("ch"), P(None, None, "ch")),
        check_vma=False,
    )
```

```python
import functools

import jax
import jax.numpy as jnp
import numpy as np
from jax import lax
from jax.experimental import pallas as pl
from jax.experimental.pallas import tpu as pltpu
from jax.sharding import PartitionSpec as P

TAPS = 128
SHORT = 3
TOK = 512
CH = 2048
POINTS = TOK + TAPS
HALF = POINTS // 2
GROUP = 16
PEERS = 32
PARTS = 4
L = CH // PARTS
LT = L // 128
MESH = pl.DeviceIdType.MESH
F32, BF16 = jnp.float32, jnp.bfloat16


def split(x):
    high = x.astype(np.float32).astype(BF16)
    return high, (x - high.astype(np.float64)).astype(np.float32).astype(BF16)


@functools.cache
def matrices():
    angle = 2 * np.pi * np.outer(np.arange(HALF) + 0.5, np.arange(POINTS)) / POINTS
    forward = np.concatenate([np.cos(angle), -np.sin(angle)])
    inverse = (2.0 / POINTS) * np.concatenate([np.cos(angle.T), -np.sin(angle.T)], axis=1)
    fh, fl = split(forward)
    cat = lambda *parts: np.concatenate(parts, axis=1)
    first, last = slice(0, TAPS), slice(TOK, POINTS)

    def back(rows):
        high, low = split(inverse[rows])
        return cat(high, high, low)

    return (
        fh,
        fl,
        cat(fh[:, first], fl[:, first]),
        cat(fh[:, last], fl[:, last]),
        cat(fh[:, first], fl[:, first], fh[:, first]),
        back(np.arange(TAPS, POINTS)),
        back(np.arange(TOK)),
        back(TAPS - np.arange(TAPS)),
    )


def dot(a, b):
    return jnp.dot(a, b, preferred_element_type=F32)


def kernel(
    proj, sf_ref, h_hbm, skip_ref, cot_hbm, m0, m1, m2, m3, m4, m5, m6, m7,
    gi_out, gl_out, gs_out,
    px, qs, ks, vs, gated, g_halo, ghat, hhat, mixed, cot, dm, dm_halo, dhat, ds, d_halo,
    yb, hb, twice, hv, f0, f1, f2, f3, f4, f5, f6, f7,
    parts, landed, xs, xr, sums, gs, gs_landed, gs_x, gs_xr, gs_sums,
    load_sem, mat_sem, h_sem, own_sem, out_sem, a2a_send, a2a_recv,
    ph_sem, gh_sem, dmh_sem, dh_sem, rs_sem, xx_sem, ag_sem, tail_sem,
):
    me = lax.axis_index("seq")
    col = lax.axis_index("ch")
    g = lax.rem(me, GROUP)
    plane = me - g
    nxt, prv = lax.rem(me + 1, PEERS), lax.rem(me + PEERS - 1, PEERS)
    across = lax.rem(me + GROUP, PEERS)
    barrier = pltpu.get_barrier_semaphore()

    def to_seq(s):
        return dict(device_id={"seq": s}, device_id_type=MESH)

    def to_ch(c):
        return dict(device_id={"ch": c}, device_id_type=MESH)

    def mate(k):
        return plane + lax.rem(g + k, GROUP)

    @pl.loop(1, GROUP)
    def _(k):
        pl.semaphore_signal(barrier, inc=1, **to_seq(mate(k)))

    for s in (nxt, prv, across):
        pl.semaphore_signal(barrier, inc=1, **to_seq(s))
    for k in range(1, 4):
        pl.semaphore_signal(barrier, inc=1, **to_ch(lax.rem(col + k, 4)))

    def lanes(c):
        return pl.ds(pl.multiple_of(c * L, L), L)

    def p_load(c):
        return pltpu.make_async_copy(proj.at[:, :, lanes(c)], px.at[c, :, 16 : 16 + TOK], load_sem.at[c])

    def h_load(c):
        return pltpu.make_async_copy(h_hbm.at[:, lanes(c)], hv.at[c], h_sem.at[c])

    mats = [
        pltpu.make_async_copy(a, b, mat_sem.at[i])
        for i, (a, b) in enumerate(zip((m0, m1, m2, m3, m4, m5, m6, m7), (f0, f1, f2, f3, f4, f5, f6, f7)))
    ]
    for c in range(PARTS):
        p_load(c).start()
        h_load(c).start()
    for m in mats:
        m.start()

    def cot_block(c, owner):
        return cot.at[c, pl.ds(pl.multiple_of(owner * 128, 128), 128)]

    def cot_own(c):
        cols = pl.ds(pl.multiple_of(col * CH + c * L, L), L)
        return pltpu.make_async_copy(cot_hbm.at[:, cols], cot_block(c, col), own_sem.at[c])

    def cot_send(c, k):
        peer = lax.rem(col + k, 4)
        cols = pl.ds(pl.multiple_of(peer * CH + c * L, L), L)
        return pltpu.make_async_remote_copy(
            src_ref=cot_hbm.at[:, cols], dst_ref=cot_block(c, col),
            send_sem=a2a_send.at[c, k - 1], recv_sem=a2a_recv.at[c, k - 1], **to_ch(peer))

    def cot_wait(c, k):
        block = cot_block(c, lax.rem(col + 4 - k, 4))
        pltpu.make_async_copy(block, block, a2a_recv.at[c, k - 1]).wait()

    def p_halo(c):
        return pltpu.make_async_remote_copy(
            src_ref=proj.at[:, TOK - 16 : TOK, lanes(c)], dst_ref=px.at[c, :, 0:16],
            send_sem=ph_sem.at[0, c], recv_sem=ph_sem.at[1, c], **to_seq(nxt))

    def gated_halo(c):
        return pltpu.make_async_remote_copy(
            src_ref=gated.at[c, TOK - TAPS : TOK], dst_ref=g_halo.at[c],
            send_sem=gh_sem.at[0, c], recv_sem=gh_sem.at[1, c], **to_seq(nxt))

    def mixed_halo(c):
        return pltpu.make_async_remote_copy(
            src_ref=dm.at[c, 0:TAPS], dst_ref=dm_halo.at[c],
            send_sem=dmh_sem.at[0, c], recv_sem=dmh_sem.at[1, c], **to_seq(prv))

    def grad_halo(c):
        return pltpu.make_async_remote_copy(
            src_ref=ds.at[c, :, 0:16], dst_ref=d_halo.at[c],
            send_sem=dh_sem.at[0, c], recv_sem=dh_sem.at[1, c], **to_seq(prv))

    def gi_store(c):
        return pltpu.make_async_copy(ds.at[c, :, 0:TOK], gi_out.at[:, :, lanes(c)], out_sem.at[c])

    pl.semaphore_wait(barrier, GROUP - 1 + 3 + 3)
    for c in range(PARTS):
        p_halo(c).start()
    for c in range(PARTS):
        cot_own(c).start()
        for k in (2, 1, 3):
            cot_send(c, k).start()

    def stream_block(c, b, l):
        rows = pl.ds(pl.multiple_of(b * 128, 128), 144)
        here = pl.ds(pl.multiple_of(b * 128, 128), 128)
        cols = pl.ds(pl.multiple_of(l * 128, 128), 128)
        wide = pl.ds(pl.multiple_of(c * L + l * 128, 128), 128)
        out = []
        for i, keep in enumerate((qs, ks, vs)):
            x = px[c, i, rows, cols].astype(F32)
            s = sf_ref[i, 0:1, wide] * x[16:144]
            s = s + sf_ref[i, 1:2, wide] * x[15:143]
            s = s + sf_ref[i, 2:3, wide] * x[14:142]
            keep[c, here, cols] = s
            out.append(s)
        gated[c, here, cols] = (out[1] * out[2]).astype(BF16)

    @pl.loop(0, PARTS)
    def _(c):
        p_load(c).wait()

        @pl.loop(0, 3 * LT)
        def _(n):
            stream_block(c, 3 - n // LT, lax.rem(n, LT))

        gated_halo(c).start()
        p_halo(c).wait_recv()

        @pl.when(me == 0)
        def _():
            px[c, :, 0:16] = jnp.zeros((3, 16, L), BF16)

        @pl.loop(0, LT)
        def _(l):
            stream_block(c, 0, l)

    for m in mats:
        m.wait()

    def products(a, b, conj):
        @pl.loop(0, HALF // 16, unroll=2)
        def _(r):
            rows = pl.ds(pl.multiple_of(r * 16, 16), 16)
            rows_i = pl.ds(pl.multiple_of(HALF + r * 16, 16), 16)
            ar, ai, br, bi = a[rows], a[rows_i], b[rows], b[rows_i]
            if conj:
                re, im = ar * br + ai * bi, ai * br - ar * bi
            else:
                re, im = ar * br - ai * bi, ar * bi + ai * br
            for value, start in ((re, 0), (im, HALF)):
                high = value.astype(BF16)
                at = pl.multiple_of(start + r * 16, 16)
                yb[pl.ds(at, 16)] = high
                yb[pl.ds(POINTS + at, 16)] = (value - high.astype(F32)).astype(BF16)

    def back(matrix):
        return dot(matrix[:, : 2 * POINTS], yb[...]) + dot(matrix[:, 2 * POINTS :], yb[0:POINTS])

    def filter_and_mix(c):
        slot, hslot = lax.rem(c, 2), lax.rem(c, 3)
        h_load(c).wait()
        h = hv[c]
        high = h.astype(BF16)
        hb[0:TAPS] = high
        hb[TAPS : 2 * TAPS] = high
        hb[2 * TAPS :] = (h - high.astype(F32)).astype(BF16)
        hhat[hslot] = dot(f4[...], hb[...])
        hhat[hslot, 0:HALF] = hhat[hslot, 0:HALF] + skip_ref[0:1, lanes(c)]
        gated_halo(c).wait_recv()

        @pl.when(me == 0)
        def _():
            g_halo[c] = jnp.zeros((TAPS, L), BF16)

        twice[0:TAPS] = g_halo[c]
        twice[TAPS:] = g_halo[c]
        own = gated[c]
        ghat[slot] = dot(f0[:, TAPS:], own) + dot(f1[:, TAPS:], own) + dot(f2[...], twice[...])
        products(ghat.at[slot], hhat.at[hslot], False)
        mixed[slot] = back(f5)

    def multiply_cotangent(c):
        slot = lax.rem(c, 2)
        cot_own(c).wait()
        for k in (2, 1, 3):
            cot_wait(c, k)

        @pl.loop(0, TOK // 16, unroll=2)
        def _(r):
            rows = pl.ds(pl.multiple_of(r * 16, 16), 16)
            up = cot[c, rows].astype(F32)
            dm[c, rows] = (up * qs[c, rows]).astype(BF16)
            ds[c, 0, rows] = (up * mixed[slot, rows]).astype(BF16)

        mixed_halo(c).start()

    def filter_gradient(c):
        slot = lax.rem(c, 2)
        own = dm[c]
        dhat[slot] = dot(f0[:, :TOK], own) + dot(f1[:, :TOK], own)
        products(ghat.at[slot], dhat.at[slot], True)
        parts[c] = back(f7)

        @pl.loop(1, GROUP)
        def _(k):
            peer = lax.rem(g + k, GROUP)
            pltpu.make_async_remote_copy(
                src_ref=parts.at[c, pl.ds(pl.multiple_of(peer * 8, 8), 8)], dst_ref=landed.at[c, k - 1],
                send_sem=rs_sem.at[0, c], recv_sem=rs_sem.at[1, c], **to_seq(plane + peer)).start()

    def gated_gradient(c):
        slot, hslot = lax.rem(c, 2), lax.rem(c, 3)
        mixed_halo(c).wait_recv()

        @pl.when(me == PEERS - 1)
        def _():
            dm_halo[c] = jnp.zeros((TAPS, L), BF16)

        twice[0:TAPS] = dm_halo[c]
        twice[TAPS:] = dm_halo[c]
        dhat[slot] = dhat[slot] + dot(f3[...], twice[...])
        products(dhat.at[slot], hhat.at[hslot], True)
        grad = back(f6)
        ds[c, 1, 0:TOK] = (grad * vs[c]).astype(BF16)
        ds[c, 2, 0:TOK] = (grad * ks[c]).astype(BF16)
        grad_halo(c).start()

    mine = pl.ds(pl.multiple_of(g * 8, 8), 8)

    def cross(c):
        return pltpu.make_async_remote_copy(
            src_ref=xs.at[c], dst_ref=xr.at[c], send_sem=xx_sem.at[0, c], recv_sem=xx_sem.at[1, c], **to_seq(across))

    def sum_plane(c):
        pltpu.make_async_copy(landed.at[c], landed.at[c], rs_sem.at[1, c]).wait()
        total = parts[c, mine]
        for k in range(GROUP - 1):
            total = total + landed[c, k]
        xs[c] = total
        cross(c).start()

    def spread(c):
        cross(c).wait_recv()
        sums[c, mine] = (xs[c] + xr[c]) * (1.0 / 128.0)

        @pl.loop(1, GROUP)
        def _(k):
            pltpu.make_async_remote_copy(
                src_ref=sums.at[c, mine], dst_ref=sums.at[c, mine],
                send_sem=ag_sem.at[0, c], recv_sem=ag_sem.at[1, c], **to_seq(mate(k))).start()

    def input_gradient(c):
        grad_halo(c).wait()
        ds[c, :, TOK : TOK + 16] = d_halo[c]

        @pl.when(me == PEERS - 1)
        def _():
            ds[c, :, TOK : TOK + 16] = jnp.zeros((3, 16, L), BF16)

        @pl.loop(0, 3 * LT)
        def _(n):
            i, l = n // LT, lax.rem(n, LT)
            cols = pl.ds(pl.multiple_of(l * 128, 128), 128)
            wide = pl.ds(pl.multiple_of(c * L + l * 128, 128), 128)
            acc = [jnp.zeros((8, 128), F32) for _ in range(SHORT)]
            for b in range(4):
                d = ds[c, i, 128 * b : 128 * b + 144, cols].astype(F32)
                p = px[c, i, 16 + 128 * b : 144 + 128 * b, cols].astype(F32)
                result = None
                for j in range(SHORT):
                    moved = d[j : j + 128]
                    term = sf_ref[i, j : j + 1, wide] * moved
                    result = term if result is None else result + term
                    acc[j] = acc[j] + jnp.sum((moved * p).reshape(16, 8, 128), axis=0)
                ds[c, i, 128 * b : 128 * b + 128, cols] = result.astype(BF16)
            for j in range(SHORT):
                gs[c * LT + l, pl.ds(3 * i + j, 1)] = jnp.sum(acc[j], axis=0, keepdims=True)

        gi_store(c).start()

    gs[...] = jnp.zeros(gs.shape, F32)
    filter_and_mix(0)

    @pl.loop(0, PARTS + 2)
    def _(s):
        @pl.when(s < PARTS)
        def _():
            multiply_cotangent(s)
            filter_gradient(s)

        @pl.when(s + 1 < PARTS)
        def _():
            filter_and_mix(s + 1)

        @pl.when(jnp.logical_and(s >= 1, s <= PARTS))
        def _():
            gated_gradient(s - 1)
            sum_plane(s - 1)

        @pl.when(s >= 2)
        def _():
            input_gradient(s - 2)
            spread(s - 2)

    @pl.loop(1, GROUP)
    def _(k):
        peer = lax.rem(g + k, GROUP)
        pltpu.make_async_remote_copy(
            src_ref=gs.at[peer], dst_ref=gs_landed.at[k - 1],
            send_sem=tail_sem.at[0], recv_sem=tail_sem.at[1], **to_seq(plane + peer)).start()

    pltpu.make_async_copy(gs_landed, gs_landed, tail_sem.at[1]).wait()
    total = gs[g]
    for k in range(GROUP - 1):
        total = total + gs_landed[k]
    gs_x[...] = total
    swap = pltpu.make_async_remote_copy(
        src_ref=gs_x, dst_ref=gs_xr, send_sem=tail_sem.at[2], recv_sem=tail_sem.at[3], **to_seq(across))
    swap.start()
    swap.wait()
    gs_sums[g] = (gs_x[...] + gs_xr[...]) * (1.0 / 128.0)

    @pl.loop(1, GROUP)
    def _(k):
        pltpu.make_async_remote_copy(
            src_ref=gs_sums.at[g], dst_ref=gs_sums.at[g],
            send_sem=tail_sem.at[4], recv_sem=tail_sem.at[5], **to_seq(mate(k))).start()

    for c in range(PARTS):
        pltpu.make_async_copy(landed.at[c], landed.at[c], ag_sem.at[1, c]).wait()
        pltpu.make_async_copy(sums.at[c], gl_out.at[:, c * L : c * L + L], h_sem.at[c]).start()
    pltpu.make_async_copy(gs_landed, gs_landed, tail_sem.at[5]).wait()
    for t in range(GROUP):
        gs_out[:, 128 * t : 128 * t + 128] = gs_sums[t]
    pltpu.make_async_copy(gs_landed, gs_landed, tail_sem.at[0]).wait()
    pltpu.make_async_copy(gs_landed, gs_landed, tail_sem.at[4]).wait()
    for c in range(PARTS):
        for k in (2, 1, 3):
            cot_send(c, k).wait_send()
        p_halo(c).wait_send()
        gated_halo(c).wait_send()
        mixed_halo(c).wait_send()
        cross(c).wait_send()
        pltpu.make_async_copy(landed.at[c], landed.at[c], rs_sem.at[0, c]).wait()
        pltpu.make_async_copy(landed.at[c], landed.at[c], ag_sem.at[0, c]).wait()
        gi_store(c).wait()
        pltpu.make_async_copy(sums.at[c], gl_out.at[:, c * L : c * L + L], h_sem.at[c]).wait()


def per_device(projected, short_filters, long_filter, skip_gain, cotangent):
    mats = [jnp.asarray(m) for m in matrices()]
    anywhere = pl.BlockSpec(memory_space=pl.ANY)
    vmem = pl.BlockSpec(memory_space=pltpu.VMEM)
    dma = pltpu.SemaphoreType.DMA
    scratch = [
        pltpu.VMEM((PARTS, 3, TOK + 16, L), BF16),
        pltpu.VMEM((PARTS, TOK, L), F32),
        pltpu.VMEM((PARTS, TOK, L), F32),
        pltpu.VMEM((PARTS, TOK, L), F32),
        pltpu.VMEM((PARTS, TOK, L), BF16),
        pltpu.VMEM((PARTS, TAPS, L), BF16),
        pltpu.VMEM((2, POINTS, L), F32),
        pltpu.VMEM((3, POINTS, L), F32),
        pltpu.VMEM((2, TOK, L), F32),
        pltpu.VMEM((PARTS, TOK, L), BF16),
        pltpu.VMEM((PARTS, TOK, L), BF16),
        pltpu.VMEM((PARTS, TAPS, L), BF16),
        pltpu.VMEM((2, POINTS, L), F32),
        pltpu.VMEM((PARTS, 3, TOK + 16, L), BF16),
        pltpu.VMEM((PARTS, 3, 16, L), BF16),
        pltpu.VMEM((2 * POINTS, L), BF16),
        pltpu.VMEM((3 * TAPS, L), BF16),
        pltpu.VMEM((2 * TAPS, L), BF16),
        pltpu.VMEM((PARTS, TAPS, L), F32),
        *[pltpu.VMEM(m.shape, BF16) for m in mats],
        pltpu.VMEM((PARTS, TAPS, L), F32),
        pltpu.VMEM((PARTS, GROUP - 1, 8, L), F32),
        pltpu.VMEM((PARTS, 8, L), F32),
        pltpu.VMEM((PARTS, 8, L), F32),
        pltpu.VMEM((PARTS, TAPS, L), F32),
        pltpu.VMEM((GROUP, 16, 128), F32),
        pltpu.VMEM((GROUP - 1, 16, 128), F32),
        pltpu.VMEM((16, 128), F32),
        pltpu.VMEM((16, 128), F32),
        pltpu.VMEM((GROUP, 16, 128), F32),
        dma((PARTS,)),
        dma((len(mats),)),
        dma((PARTS,)),
        dma((PARTS,)),
        dma((PARTS,)),
        dma((PARTS, 3)),
        dma((PARTS, 3)),
        *[dma((2, PARTS)) for _ in range(7)],
        dma((6,)),
    ]
    grad_input, grad_long, grad_short = pl.pallas_call(
        kernel,
        out_shape=(
            jax.ShapeDtypeStruct((3, TOK, CH), BF16),
            jax.ShapeDtypeStruct((TAPS, CH), F32),
            jax.ShapeDtypeStruct((16, CH), F32),
        ),
        in_specs=[anywhere, vmem, anywhere, vmem, anywhere] + [anywhere] * len(mats),
        out_specs=(anywhere, anywhere, vmem),
        scratch_shapes=scratch,
        compiler_params=pltpu.CompilerParams(collective_id=0, has_side_effects=True, vmem_limit_bytes=62 << 20),
        cost_estimate=pl.CostEstimate(flops=20 * 10**9, bytes_accessed=24 * 10**6, transcendentals=0),
    )(projected, short_filters, long_filter, skip_gain[None], cotangent, *mats)
    return grad_input, grad_long, grad_long[0], grad_short[:9].reshape(3, SHORT, CH)


def solution(mesh):
    placed = (
        P(None, "seq", "ch"),
        P(None, None, "ch"),
        P(None, "ch"),
        P("ch"),
        P(("seq", "ch"), None),
    )
    return jax.shard_map(
        per_device,
        mesh=mesh,
        in_specs=placed,
        out_specs=(P(None, "seq", "ch"), P(None, "ch"), P("ch"), P(None, None, "ch")),
        check_vma=False,
    )
```

```python
import functools

import jax
import jax.numpy as jnp
import numpy as np
from jax import lax
from jax.experimental import pallas as pl
from jax.experimental.pallas import tpu as pltpu
from jax.sharding import PartitionSpec as P

TAPS = 128
SHORT = 3
TOK = 512
CH = 2048
POINTS = TOK + TAPS
HALF = POINTS // 2
GROUP = 16
PEERS = 32
PARTS = 4
L = CH // PARTS
LT = L // 128
MESH = pl.DeviceIdType.MESH
F32, BF16 = jnp.float32, jnp.bfloat16


def split(x):
    high = x.astype(np.float32).astype(BF16)
    return high, (x - high.astype(np.float64)).astype(np.float32).astype(BF16)


@functools.cache
def matrices():
    angle = 2 * np.pi * np.outer(np.arange(HALF) + 0.5, np.arange(POINTS)) / POINTS
    forward = np.concatenate([np.cos(angle), -np.sin(angle)])
    inverse = (2.0 / POINTS) * np.concatenate([np.cos(angle.T), -np.sin(angle.T)], axis=1)
    fh, fl = split(forward)
    cat = lambda *parts: np.concatenate(parts, axis=1)
    first, last = slice(0, TAPS), slice(TOK, POINTS)

    def back(rows):
        high, low = split(inverse[rows])
        return cat(high, high, low)

    return (
        fh,
        fl,
        cat(fh[:, first], fl[:, first]),
        cat(fh[:, last], fl[:, last]),
        cat(fh[:, first], fl[:, first], fh[:, first]),
        back(np.arange(TAPS, POINTS)),
        back(np.arange(TOK)),
        back(TAPS - np.arange(TAPS)),
    )


def dot(a, b):
    return jnp.dot(a, b, preferred_element_type=F32)


def kernel(
    proj, sf_ref, h_hbm, skip_ref, cot_hbm, m0, m1, m2, m3, m4, m5, m6, m7,
    d_out, gl_out, gs_out,
    px, tip, p_halo_ref, qs, ks, vs, gated, g_halo, ghat, hhat, mixed, cot, dm, dm_halo, dhat, ds, d_halo,
    yb, hb, twice, hv, f0, f1, f2, f3, f4, f5, f6, f7,
    parts, landed, xs, xr, sums, gs, gs_landed, gs_sums,
    load_sem, mat_sem, h_sem, own_sem, out_sem, halo_out_sem, a2a_send, a2a_recv,
    ph_sem, gh_sem, dmh_sem, dh_sem, rs_sem, xx_sem, ag_sem, tail_sem,
):
    me = lax.axis_index("seq")
    col = lax.axis_index("ch")
    g = lax.rem(me, GROUP)
    plane = me - g
    nxt, prv = lax.rem(me + 1, PEERS), lax.rem(me + PEERS - 1, PEERS)
    across = lax.rem(me + GROUP, PEERS)
    barrier = pltpu.get_barrier_semaphore()

    def to_seq(s):
        return dict(device_id={"seq": s}, device_id_type=MESH)

    def to_ch(c):
        return dict(device_id={"ch": c}, device_id_type=MESH)

    def mate(k):
        return plane + lax.rem(g + k, GROUP)

    @pl.loop(1, PEERS)
    def _(k):
        pl.semaphore_signal(barrier, inc=1, **to_seq(lax.rem(me + k, PEERS)))

    for k in range(1, 4):
        pl.semaphore_signal(barrier, inc=1, **to_ch(lax.rem(col + k, 4)))

    def lanes(c):
        return pl.ds(pl.multiple_of(c * L, L), L)

    def p_load(c):
        return pltpu.make_async_copy(proj.at[:, :, lanes(c)], px.at[c, :, 16 : 16 + TOK], load_sem.at[c])

    def h_load(c):
        return pltpu.make_async_copy(h_hbm.at[:, lanes(c)], hv.at[c], h_sem.at[c])

    mats = [
        pltpu.make_async_copy(a, b, mat_sem.at[i])
        for i, (a, b) in enumerate(zip((m0, m1, m2, m3, m4, m5, m6, m7), (f0, f1, f2, f3, f4, f5, f6, f7)))
    ]
    for c in range(PARTS):
        p_load(c).start()
        h_load(c).start()
    for m in mats:
        m.start()

    def cot_block(c, owner):
        return cot.at[c, pl.ds(pl.multiple_of(owner * 128, 128), 128)]

    def cot_own(c):
        cols = pl.ds(pl.multiple_of(col * CH + c * L, L), L)
        return pltpu.make_async_copy(cot_hbm.at[:, cols], cot_block(c, col), own_sem.at[c])

    def cot_send(c, k):
        peer = lax.rem(col + k, 4)
        cols = pl.ds(pl.multiple_of(peer * CH + c * L, L), L)
        return pltpu.make_async_remote_copy(
            src_ref=cot_hbm.at[:, cols], dst_ref=cot_block(c, col),
            send_sem=a2a_send.at[c, k - 1], recv_sem=a2a_recv.at[c, k - 1], **to_ch(peer))

    def cot_wait(c, k):
        block = cot_block(c, lax.rem(col + 4 - k, 4))
        pltpu.make_async_copy(block, block, a2a_recv.at[c, k - 1]).wait()

    def p_halo(c):
        return pltpu.make_async_remote_copy(
            src_ref=tip.at[c], dst_ref=p_halo_ref.at[c],
            send_sem=ph_sem.at[0, c], recv_sem=ph_sem.at[1, c], **to_seq(nxt))

    def gated_halo(c):
        return pltpu.make_async_remote_copy(
            src_ref=gated.at[c, TOK - TAPS : TOK], dst_ref=g_halo.at[c],
            send_sem=gh_sem.at[0, c], recv_sem=gh_sem.at[1, c], **to_seq(nxt))

    def mixed_halo(c):
        return pltpu.make_async_remote_copy(
            src_ref=dm.at[c, 0:TAPS], dst_ref=dm_halo.at[c],
            send_sem=dmh_sem.at[0, c], recv_sem=dmh_sem.at[1, c], **to_seq(prv))

    def grad_halo(c):
        return pltpu.make_async_remote_copy(
            src_ref=ds.at[c, :, 0:16], dst_ref=d_halo.at[c],
            send_sem=dh_sem.at[0, c], recv_sem=dh_sem.at[1, c], **to_seq(prv))

    def d_store(c):
        return pltpu.make_async_copy(ds.at[c, :, 0:TOK], d_out.at[:, 0:TOK, lanes(c)], out_sem.at[c])

    def halo_store(c):
        return pltpu.make_async_copy(d_halo.at[c], d_out.at[:, TOK : TOK + 16, lanes(c)], halo_out_sem.at[c])

    def cot_start(c):
        cot_own(c).start()
        for k in (2, 1, 3):
            cot_send(c, k).start()

    has_next, has_previous = me < PEERS - 1, me > 0

    pl.semaphore_wait(barrier, PEERS - 1 + 3)
    cot_start(0)

    def stream_block(c, b, l):
        rows = pl.ds(pl.multiple_of(b * 128, 128), 144)
        here = pl.ds(pl.multiple_of(b * 128, 128), 128)
        cols = pl.ds(pl.multiple_of(l * 128, 128), 128)
        wide = pl.ds(pl.multiple_of(c * L + l * 128, 128), 128)
        out = []
        for i, keep in enumerate((qs, ks, vs)):
            x = px[c, i, rows, cols].astype(F32)
            s = sf_ref[i, 0:1, wide] * x[16:144]
            s = s + sf_ref[i, 1:2, wide] * x[15:143]
            s = s + sf_ref[i, 2:3, wide] * x[14:142]
            keep[c, here, cols] = s
            out.append(s)
        gated[c, here, cols] = (out[1] * out[2]).astype(BF16)

    @pl.loop(0, PARTS)
    def _(c):
        p_load(c).wait()
        last = [px[c, i, TOK : TOK + 16].astype(F32)[14:16] for i in range(3)]
        tip[c] = jnp.concatenate(last + [jnp.zeros((10, L), F32)], axis=0).astype(BF16)

        @pl.when(has_next)
        def _():
            p_halo(c).start()

    @pl.loop(0, PARTS)
    def _(c):
        @pl.loop(0, 3 * LT)
        def _(n):
            stream_block(c, 3 - n // LT, lax.rem(n, LT))

        @pl.when(has_next)
        def _():
            gated_halo(c).start()

    cot_start(1)

    @pl.loop(0, PARTS)
    def _(c):
        @pl.when(has_previous)
        def _():
            p_halo(c).wait_recv()

        @pl.when(me == 0)
        def _():
            p_halo_ref[c] = jnp.zeros((16, L), BF16)

        before = p_halo_ref[c].astype(F32)
        for i in range(3):
            rows = jnp.concatenate([jnp.zeros((14, L), F32), before[2 * i : 2 * i + 2]], axis=0)
            px[c, i, 0:16] = rows.astype(BF16)

        @pl.loop(0, LT)
        def _(l):
            stream_block(c, 0, l)

    for m in mats:
        m.wait()

    def products(a, b, conj):
        @pl.loop(0, HALF // 16, unroll=2)
        def _(r):
            rows = pl.ds(pl.multiple_of(r * 16, 16), 16)
            rows_i = pl.ds(pl.multiple_of(HALF + r * 16, 16), 16)
            ar, ai, br, bi = a[rows], a[rows_i], b[rows], b[rows_i]
            if conj:
                re, im = ar * br + ai * bi, ai * br - ar * bi
            else:
                re, im = ar * br - ai * bi, ar * bi + ai * br
            for value, start in ((re, 0), (im, HALF)):
                high = value.astype(BF16)
                at = pl.multiple_of(start + r * 16, 16)
                yb[pl.ds(at, 16)] = high
                yb[pl.ds(POINTS + at, 16)] = (value - high.astype(F32)).astype(BF16)

    def back(matrix):
        return dot(matrix[:, : 2 * POINTS], yb[...]) + dot(matrix[:, 2 * POINTS :], yb[0:POINTS])

    def filter_and_mix(c):
        slot, hslot = lax.rem(c, 2), lax.rem(c, 3)
        h_load(c).wait()
        h = hv[c]
        high = h.astype(BF16)
        hb[0:TAPS] = high
        hb[TAPS : 2 * TAPS] = high
        hb[2 * TAPS :] = (h - high.astype(F32)).astype(BF16)
        hhat[hslot] = dot(f4[...], hb[...])
        hhat[hslot, 0:HALF] = hhat[hslot, 0:HALF] + skip_ref[0:1, lanes(c)]
        @pl.when(has_previous)
        def _():
            gated_halo(c).wait_recv()

        @pl.when(me == 0)
        def _():
            g_halo[c] = jnp.zeros((TAPS, L), BF16)

        twice[0:TAPS] = g_halo[c]
        twice[TAPS:] = g_halo[c]
        own = gated[c]
        ghat[slot] = dot(f0[:, TAPS:], own) + dot(f1[:, TAPS:], own) + dot(f2[...], twice[...])
        products(ghat.at[slot], hhat.at[hslot], False)
        mixed[slot] = back(f5)

    def multiply_cotangent(c):
        slot = lax.rem(c, 2)
        cot_own(c).wait()
        for k in (2, 1, 3):
            cot_wait(c, k)

        @pl.loop(0, TOK // 16, unroll=2)
        def _(r):
            rows = pl.ds(pl.multiple_of(r * 16, 16), 16)
            up = cot[c, rows].astype(F32)
            dm[c, rows] = (up * qs[c, rows]).astype(BF16)
            ds[c, 0, rows] = (up * mixed[slot, rows]).astype(BF16)

        @pl.when(has_previous)
        def _():
            mixed_halo(c).start()

    def filter_gradient(c):
        slot = lax.rem(c, 2)
        own = dm[c]
        dhat[slot] = dot(f0[:, :TOK], own) + dot(f1[:, :TOK], own)
        products(ghat.at[slot], dhat.at[slot], True)
        parts[c] = back(f7)

        @pl.loop(1, GROUP)
        def _(k):
            peer = lax.rem(g + k, GROUP)
            pltpu.make_async_remote_copy(
                src_ref=parts.at[c, pl.ds(pl.multiple_of(peer * 8, 8), 8)], dst_ref=landed.at[c, k - 1],
                send_sem=rs_sem.at[0, c], recv_sem=rs_sem.at[1, c], **to_seq(plane + peer)).start()

    def gated_gradient(c):
        slot, hslot = lax.rem(c, 2), lax.rem(c, 3)
        @pl.when(has_next)
        def _():
            mixed_halo(c).wait_recv()

        @pl.when(me == PEERS - 1)
        def _():
            dm_halo[c] = jnp.zeros((TAPS, L), BF16)

        twice[0:TAPS] = dm_halo[c]
        twice[TAPS:] = dm_halo[c]
        dhat[slot] = dhat[slot] + dot(f3[...], twice[...])
        products(dhat.at[slot], hhat.at[hslot], True)
        grad = back(f6)
        ds[c, 1, 0:TOK] = (grad * vs[c]).astype(BF16)
        ds[c, 2, 0:TOK] = (grad * ks[c]).astype(BF16)
        d_store(c).start()

        @pl.when(has_previous)
        def _():
            grad_halo(c).start()

    mine = pl.ds(pl.multiple_of(g * 8, 8), 8)

    def cross(c):
        return pltpu.make_async_remote_copy(
            src_ref=xs.at[c], dst_ref=xr.at[c], send_sem=xx_sem.at[0, c], recv_sem=xx_sem.at[1, c], **to_seq(across))

    def sum_plane(c):
        pltpu.make_async_copy(landed.at[c], landed.at[c], rs_sem.at[1, c]).wait()
        total = parts[c, mine]
        for k in range(GROUP - 1):
            total = total + landed[c, k]
        xs[c] = total
        cross(c).start()

    def spread(c):
        cross(c).wait_recv()
        sums[c, mine] = (xs[c] + xr[c]) * (1.0 / 128.0)

        @pl.loop(1, GROUP)
        def _(k):
            pltpu.make_async_remote_copy(
                src_ref=sums.at[c, mine], dst_ref=sums.at[c, mine],
                send_sem=ag_sem.at[0, c], recv_sem=ag_sem.at[1, c], **to_seq(mate(k))).start()

    def short_gradient(c):
        @pl.when(has_next)
        def _():
            grad_halo(c).wait_recv()

        @pl.when(me == PEERS - 1)
        def _():
            d_halo[c] = jnp.zeros((3, 16, L), BF16)

        halo_store(c).start()
        ds[c, :, TOK : TOK + 16] = d_halo[c]

        @pl.loop(0, 3 * LT)
        def _(n):
            i, l = n // LT, lax.rem(n, LT)
            cols = pl.ds(pl.multiple_of(l * 128, 128), 128)
            acc = [jnp.zeros((8, 128), F32) for _ in range(SHORT)]
            for b in range(4):
                d = ds[c, i, 128 * b : 128 * b + 144, cols].astype(F32)
                p = px[c, i, 16 + 128 * b : 144 + 128 * b, cols].astype(F32)
                for j in range(SHORT):
                    acc[j] = acc[j] + jnp.sum((d[j : j + 128] * p).reshape(16, 8, 128), axis=0)
            for j in range(SHORT):
                gs[c * LT + l, pl.ds(3 * i + j, 1)] = jnp.sum(acc[j], axis=0, keepdims=True)

    gs[...] = jnp.zeros(gs.shape, F32)
    filter_and_mix(0)

    @pl.loop(0, PARTS + 2)
    def _(s):
        @pl.when(s + 2 < PARTS)
        def _():
            cot_start(s + 2)

        @pl.when(s < PARTS)
        def _():
            multiply_cotangent(s)
            filter_gradient(s)

        @pl.when(s + 1 < PARTS)
        def _():
            filter_and_mix(s + 1)

        @pl.when(jnp.logical_and(s >= 1, s <= PARTS))
        def _():
            gated_gradient(s - 1)
            sum_plane(s - 1)

        @pl.when(s >= 2)
        def _():
            spread(s - 2)
            short_gradient(s - 2)

    @pl.loop(1, PEERS)
    def _(k):
        peer = lax.rem(me + k, PEERS)
        pltpu.make_async_remote_copy(
            src_ref=gs.at[lax.rem(peer, GROUP)], dst_ref=gs_landed.at[me],
            send_sem=tail_sem.at[0], recv_sem=tail_sem.at[1], **to_seq(peer)).start()

    gs_landed[me] = gs[g]
    others = gs_landed.at[0 : PEERS - 1]
    mates = gs_landed.at[0 : GROUP - 1]
    pltpu.make_async_copy(others, others, tail_sem.at[1]).wait()
    total = gs_landed[0]
    for k in range(1, PEERS):
        total = total + gs_landed[k]
    gs_sums[g] = total * (1.0 / 128.0)

    @pl.loop(1, GROUP)
    def _(k):
        pltpu.make_async_remote_copy(
            src_ref=gs_sums.at[g], dst_ref=gs_sums.at[g],
            send_sem=tail_sem.at[2], recv_sem=tail_sem.at[3], **to_seq(mate(k))).start()

    def gl_store(c):
        return pltpu.make_async_copy(sums.at[c], gl_out.at[:, lanes(c)], h_sem.at[c])

    @pl.loop(0, PARTS)
    def _(c):
        pltpu.make_async_copy(landed.at[c], landed.at[c], ag_sem.at[1, c]).wait()
        gl_store(c).start()
        for k in (2, 1, 3):
            cot_send(c, k).wait_send()

        @pl.when(has_next)
        def _():
            p_halo(c).wait_send()
            gated_halo(c).wait_send()

        @pl.when(has_previous)
        def _():
            mixed_halo(c).wait_send()
            grad_halo(c).wait_send()

        cross(c).wait_send()
        pltpu.make_async_copy(landed.at[c], landed.at[c], rs_sem.at[0, c]).wait()
        pltpu.make_async_copy(landed.at[c], landed.at[c], ag_sem.at[0, c]).wait()
        d_store(c).wait()
        halo_store(c).wait()
        gl_store(c).wait()

    pltpu.make_async_copy(others, others, tail_sem.at[0]).wait()
    pltpu.make_async_copy(mates, mates, tail_sem.at[3]).wait()
    pltpu.make_async_copy(mates, mates, tail_sem.at[2]).wait()
    gs_out[...] = gs_sums[...]


def finish_kernel(sf_ref, d_ref, gl_ref, top_ref, gs_ref, gi_out, gl_out, skip_out, gs_out):
    c, i = pl.program_id(0), pl.program_id(1)

    @pl.loop(0, 4 * LT)
    def _(n):
        l, b = n // 4, lax.rem(n, 4)
        cols = pl.ds(pl.multiple_of(l * 128, 128), 128)
        wide = pl.ds(pl.multiple_of(c * L + l * 128, 128), 128)
        d = d_ref[0, pl.ds(pl.multiple_of(b * 128, 128), 144), cols].astype(F32)
        result = sf_ref[i, 0:1, wide] * d[0:128]
        for j in range(1, SHORT):
            result = result + sf_ref[i, j : j + 1, wide] * d[j : j + 128]
        gi_out[0, pl.ds(pl.multiple_of(b * 128, 128), 128), cols] = result.astype(BF16)

    @pl.when(i == 0)
    def _():
        gl_out[...] = gl_ref[...]

    @pl.when(jnp.logical_and(c == 0, i == 0))
    def _():
        skip_out[...] = top_ref[0]
        for stream in range(3):
            for j in range(SHORT):
                row = 3 * stream + j
                gs_out[stream, j : j + 1] = jnp.concatenate(
                    [gs_ref[t, row : row + 1] for t in range(GROUP)], axis=1)


def finish(short_filters, d, gl, gs):
    whole = lambda shape: pl.BlockSpec(shape, lambda c, i: (0,) * len(shape))
    return pl.pallas_call(
        finish_kernel,
        grid=(PARTS, 3),
        out_shape=(
            jax.ShapeDtypeStruct((3, TOK, CH), BF16),
            jax.ShapeDtypeStruct((TAPS, CH), F32),
            jax.ShapeDtypeStruct((CH,), F32),
            jax.ShapeDtypeStruct((3, SHORT, CH), F32),
        ),
        in_specs=[
            whole((3, SHORT, CH)),
            pl.BlockSpec((1, TOK + 16, L), lambda c, i: (i, 0, c)),
            pl.BlockSpec((TAPS, L), lambda c, i: (0, c)),
            whole((8, CH)),
            whole((GROUP, 16, 128)),
        ],
        out_specs=(
            pl.BlockSpec((1, TOK, L), lambda c, i: (i, 0, c)),
            pl.BlockSpec((TAPS, L), lambda c, i: (0, c)),
            whole((CH,)),
            whole((3, SHORT, CH)),
        ),
        compiler_params=pltpu.CompilerParams(vmem_limit_bytes=24 << 20),
        cost_estimate=pl.CostEstimate(flops=2 * 10**7, bytes_accessed=16 * 10**6, transcendentals=0),
    )(short_filters, d, gl, gl, gs)


def per_device(projected, short_filters, long_filter, skip_gain, cotangent):
    mats = [jnp.asarray(m) for m in matrices()]
    anywhere = pl.BlockSpec(memory_space=pl.ANY)
    vmem = pl.BlockSpec(memory_space=pltpu.VMEM)
    dma = pltpu.SemaphoreType.DMA
    scratch = [
        pltpu.VMEM((PARTS, 3, TOK + 16, L), BF16),
        pltpu.VMEM((PARTS, 16, L), BF16),
        pltpu.VMEM((PARTS, 16, L), BF16),
        pltpu.VMEM((PARTS, TOK, L), F32),
        pltpu.VMEM((PARTS, TOK, L), F32),
        pltpu.VMEM((PARTS, TOK, L), F32),
        pltpu.VMEM((PARTS, TOK, L), BF16),
        pltpu.VMEM((PARTS, TAPS, L), BF16),
        pltpu.VMEM((2, POINTS, L), F32),
        pltpu.VMEM((3, POINTS, L), F32),
        pltpu.VMEM((2, TOK, L), F32),
        pltpu.VMEM((PARTS, TOK, L), BF16),
        pltpu.VMEM((PARTS, TOK, L), BF16),
        pltpu.VMEM((PARTS, TAPS, L), BF16),
        pltpu.VMEM((2, POINTS, L), F32),
        pltpu.VMEM((PARTS, 3, TOK + 16, L), BF16),
        pltpu.VMEM((PARTS, 3, 16, L), BF16),
        pltpu.VMEM((2 * POINTS, L), BF16),
        pltpu.VMEM((3 * TAPS, L), BF16),
        pltpu.VMEM((2 * TAPS, L), BF16),
        pltpu.VMEM((PARTS, TAPS, L), F32),
        *[pltpu.VMEM(m.shape, BF16) for m in mats],
        pltpu.VMEM((PARTS, TAPS, L), F32),
        pltpu.VMEM((PARTS, GROUP - 1, 8, L), F32),
        pltpu.VMEM((PARTS, 8, L), F32),
        pltpu.VMEM((PARTS, 8, L), F32),
        pltpu.VMEM((PARTS, TAPS, L), F32),
        pltpu.VMEM((GROUP, 16, 128), F32),
        pltpu.VMEM((PEERS, 16, 128), F32),
        pltpu.VMEM((GROUP, 16, 128), F32),
        dma((PARTS,)),
        dma((len(mats),)),
        dma((PARTS,)),
        dma((PARTS,)),
        dma((PARTS,)),
        dma((PARTS,)),
        dma((PARTS, 3)),
        dma((PARTS, 3)),
        *[dma((2, PARTS)) for _ in range(7)],
        dma((4,)),
    ]
    d, gl, gs = pl.pallas_call(
        kernel,
        out_shape=(
            jax.ShapeDtypeStruct((3, TOK + 16, CH), BF16),
            jax.ShapeDtypeStruct((TAPS, CH), F32),
            jax.ShapeDtypeStruct((GROUP, 16, 128), F32),
        ),
        in_specs=[anywhere, vmem, anywhere, vmem, anywhere] + [anywhere] * len(mats),
        out_specs=(anywhere, anywhere, vmem),
        scratch_shapes=scratch,
        compiler_params=pltpu.CompilerParams(collective_id=0, has_side_effects=True, vmem_limit_bytes=62 << 20),
        cost_estimate=pl.CostEstimate(flops=20 * 10**9, bytes_accessed=24 * 10**6, transcendentals=0),
    )(projected, short_filters, long_filter, skip_gain[None], cotangent, *mats)
    return finish(short_filters, d, gl, gs)


def solution(mesh):
    placed = (
        P(None, "seq", "ch"),
        P(None, None, "ch"),
        P(None, "ch"),
        P("ch"),
        P(("seq", "ch"), None),
    )
    return jax.shard_map(
        per_device,
        mesh=mesh,
        in_specs=placed,
        out_specs=(P(None, "seq", "ch"), P(None, "ch"), P("ch"), P(None, None, "ch")),
        check_vma=False,
    )
```

```python
import functools

import jax
import jax.numpy as jnp
import numpy as np
from jax import lax
from jax.experimental import pallas as pl
from jax.experimental.pallas import tpu as pltpu
from jax.sharding import PartitionSpec as P

TAPS = 128
SHORT = 3
TOK = 512
CH = 2048
POINTS = TOK + TAPS
HALF = POINTS // 2
GROUP = 16
PEERS = 32
PARTS = 4
L = CH // PARTS
LT = L // 128
MESH = pl.DeviceIdType.MESH
F32, BF16 = jnp.float32, jnp.bfloat16


def split(x):
    high = x.astype(np.float32).astype(BF16)
    return high, (x - high.astype(np.float64)).astype(np.float32).astype(BF16)


@functools.cache
def matrices():
    angle = 2 * np.pi * np.outer(np.arange(HALF) + 0.5, np.arange(POINTS)) / POINTS
    forward = np.concatenate([np.cos(angle), -np.sin(angle)])
    inverse = (2.0 / POINTS) * np.concatenate([np.cos(angle.T), -np.sin(angle.T)], axis=1)
    fh, fl = split(forward)
    cat = lambda *parts: np.concatenate(parts, axis=1)
    first, last = slice(0, TAPS), slice(TOK, POINTS)

    def back(rows):
        high, low = split(inverse[rows])
        return cat(high, high, low)

    return (
        fh,
        fl,
        cat(fh[:, first], fl[:, first]),
        cat(fh[:, last], fl[:, last]),
        cat(fh[:, first], fl[:, first], fh[:, first]),
        back(np.arange(TAPS, POINTS)),
        back(np.arange(TOK)),
        back(TAPS - np.arange(TAPS)),
    )


def dot(a, b):
    return jnp.dot(a, b, preferred_element_type=F32)


def kernel(
    proj, sf_ref, h_hbm, skip_ref, cot_hbm, m0, m1, m2, m3, m4, m5, m6, m7,
    d_out, gl_out, gs_out,
    px, tip, p_halo_ref, qs, ks, vs, gated, g_halo, ghat, hhat, mixed, cot, dm, dm_halo, dhat, ds, d_halo,
    yb, hb, twice, line, hv, f0, f1, f2, f3, f4, f5, f6, f7,
    parts, landed, xs, xr, sums, gs, gs_landed, gs_sums,
    load_sem, mat_sem, h_sem, own_sem, out_sem, halo_out_sem, a2a_send, a2a_recv,
    ph_sem, gh_sem, dmh_sem, dh_sem, rs_sem, xx_sem, ag_sem, tail_sem,
):
    me = lax.axis_index("seq")
    col = lax.axis_index("ch")
    g = lax.rem(me, GROUP)
    plane = me - g
    nxt, prv = lax.rem(me + 1, PEERS), lax.rem(me + PEERS - 1, PEERS)
    across = lax.rem(me + GROUP, PEERS)
    barrier = pltpu.get_barrier_semaphore()

    def to_seq(s):
        return dict(device_id={"seq": s}, device_id_type=MESH)

    def to_ch(c):
        return dict(device_id={"ch": c}, device_id_type=MESH)

    def mate(k):
        return plane + lax.rem(g + k, GROUP)

    @pl.loop(1, PEERS)
    def _(k):
        pl.semaphore_signal(barrier, inc=1, **to_seq(lax.rem(me + k, PEERS)))

    for k in range(1, 4):
        pl.semaphore_signal(barrier, inc=1, **to_ch(lax.rem(col + k, 4)))

    def lanes(c):
        return pl.ds(pl.multiple_of(c * L, L), L)

    def p_load(c):
        return pltpu.make_async_copy(proj.at[:, :, lanes(c)], px.at[c, :, 16 : 16 + TOK], load_sem.at[c])

    def h_load(c):
        return pltpu.make_async_copy(h_hbm.at[:, lanes(c)], hv.at[c], h_sem.at[c])

    mats = [
        pltpu.make_async_copy(a, b, mat_sem.at[i])
        for i, (a, b) in enumerate(zip((m0, m1, m2, m3, m4, m5, m6, m7), (f0, f1, f2, f3, f4, f5, f6, f7)))
    ]
    for c in range(PARTS):
        p_load(c).start()
        h_load(c).start()
    for m in mats:
        m.start()

    def cot_block(c, owner):
        return cot.at[c, pl.ds(pl.multiple_of(owner * 128, 128), 128)]

    def cot_own(c):
        cols = pl.ds(pl.multiple_of(col * CH + c * L, L), L)
        return pltpu.make_async_copy(cot_hbm.at[:, cols], cot_block(c, col), own_sem.at[c])

    def cot_send(c, k):
        peer = lax.rem(col + k, 4)
        cols = pl.ds(pl.multiple_of(peer * CH + c * L, L), L)
        return pltpu.make_async_remote_copy(
            src_ref=cot_hbm.at[:, cols], dst_ref=cot_block(c, col),
            send_sem=a2a_send.at[c, k - 1], recv_sem=a2a_recv.at[c, k - 1], **to_ch(peer))

    def cot_wait(c, k):
        block = cot_block(c, lax.rem(col + 4 - k, 4))
        pltpu.make_async_copy(block, block, a2a_recv.at[c, k - 1]).wait()

    def p_halo(c):
        return pltpu.make_async_remote_copy(
            src_ref=tip.at[c], dst_ref=p_halo_ref.at[c],
            send_sem=ph_sem.at[0, c], recv_sem=ph_sem.at[1, c], **to_seq(nxt))

    def gated_halo(c):
        return pltpu.make_async_remote_copy(
            src_ref=gated.at[c, TOK - TAPS : TOK], dst_ref=g_halo.at[c],
            send_sem=gh_sem.at[0, c], recv_sem=gh_sem.at[1, c], **to_seq(nxt))

    def mixed_halo(c):
        return pltpu.make_async_remote_copy(
            src_ref=dm.at[c, 0:TAPS], dst_ref=dm_halo.at[c],
            send_sem=dmh_sem.at[0, c], recv_sem=dmh_sem.at[1, c], **to_seq(prv))

    def grad_halo(c):
        return pltpu.make_async_remote_copy(
            src_ref=ds.at[c, :, 0:16], dst_ref=d_halo.at[c],
            send_sem=dh_sem.at[0, c], recv_sem=dh_sem.at[1, c], **to_seq(prv))

    def d_store(c):
        return pltpu.make_async_copy(ds.at[c, :, 0:TOK], d_out.at[:, 0:TOK, lanes(c)], out_sem.at[c])

    def halo_store(c):
        return pltpu.make_async_copy(d_halo.at[c], d_out.at[:, TOK : TOK + 16, lanes(c)], halo_out_sem.at[c])

    def cot_start(c):
        cot_own(c).start()
        for k in (2, 1, 3):
            cot_send(c, k).start()

    has_next, has_previous = me < PEERS - 1, me > 0

    def stream_rows(c, l):
        cols = pl.ds(pl.multiple_of(l * 128, 128), 128)
        wide = pl.ds(pl.multiple_of(c * L + l * 128, 128), 128)
        for i in range(3):
            line[i] = px[c, i, :, cols].astype(F32)
        taps = [[sf_ref[i, j : j + 1, wide] for j in range(SHORT)] for i in range(3)]

        @pl.loop(0, TOK // 64, unroll=4)
        def _(b):
            here = pl.ds(pl.multiple_of(b * 64, 64), 64)
            out = []
            for i, keep in enumerate((qs, ks, vs)):
                s = taps[i][0] * line[i, pl.ds(b * 64 + 16, 64)]
                s = s + taps[i][1] * line[i, pl.ds(b * 64 + 15, 64)]
                s = s + taps[i][2] * line[i, pl.ds(b * 64 + 14, 64)]
                keep[c, here, cols] = s
                out.append(s)
            gated[c, here, cols] = (out[1] * out[2]).astype(BF16)

    pl.semaphore_wait(barrier, PEERS - 1 + 3)
    cot_start(0)

    @pl.loop(0, PARTS)
    def _(c):
        p_load(c).wait()
        px[c, :, 0:16] = jnp.zeros((3, 16, L), BF16)
        last = [px[c, i, TOK : TOK + 16].astype(F32)[14:16] for i in range(3)]
        tip[c] = jnp.concatenate(last + [jnp.zeros((10, L), F32)], axis=0).astype(BF16)

        @pl.when(has_next)
        def _():
            p_halo(c).start()

        @pl.loop(0, LT)
        def _(l):
            stream_rows(c, l)

        @pl.when(jnp.logical_and(has_next, c == 0))
        def _():
            gated_halo(c).start()

    @pl.when(has_next)
    def _():
        gated_halo(1).start()

    cot_start(1)
    for m in mats:
        m.wait()

    def filter_transform(c):
        h_load(c).wait()
        h = hv[c]
        high = h.astype(BF16)
        hb[0:TAPS] = high
        hb[TAPS : 2 * TAPS] = high
        hb[2 * TAPS :] = (h - high.astype(F32)).astype(BF16)
        hslot = lax.rem(c, 3)
        hhat[hslot] = dot(f4[...], hb[...])
        hhat[hslot, 0:HALF] = hhat[hslot, 0:HALF] + skip_ref[0:1, lanes(c)]

    filter_transform(0)

    @pl.loop(0, PARTS)
    def _(c):
        @pl.when(has_previous)
        def _():
            p_halo(c).wait_recv()

        @pl.when(me == 0)
        def _():
            p_halo_ref[c] = jnp.zeros((16, L), BF16)

        before = p_halo_ref[c].astype(F32)
        out = []
        for i, keep in enumerate((qs, ks, vs)):
            x = jnp.concatenate([before[2 * i : 2 * i + 2], px[c, i, 16:32].astype(F32)], axis=0)
            s = sf_ref[i, 0:1, lanes(c)] * x[2:18]
            s = s + sf_ref[i, 1:2, lanes(c)] * x[1:17]
            s = s + sf_ref[i, 2:3, lanes(c)] * x[0:16]
            keep[c, 0:16] = s
            out.append(s)
        gated[c, 0:16] = (out[1] * out[2]).astype(BF16)

    def products(a, b, conj):
        @pl.loop(0, HALF // 16, unroll=2)
        def _(r):
            rows = pl.ds(pl.multiple_of(r * 16, 16), 16)
            rows_i = pl.ds(pl.multiple_of(HALF + r * 16, 16), 16)
            ar, ai, br, bi = a[rows], a[rows_i], b[rows], b[rows_i]
            if conj:
                re, im = ar * br + ai * bi, ai * br - ar * bi
            else:
                re, im = ar * br - ai * bi, ar * bi + ai * br
            for value, start in ((re, 0), (im, HALF)):
                high = value.astype(BF16)
                at = pl.multiple_of(start + r * 16, 16)
                yb[pl.ds(at, 16)] = high
                yb[pl.ds(POINTS + at, 16)] = (value - high.astype(F32)).astype(BF16)

    def back(matrix):
        return dot(matrix[:, : 2 * POINTS], yb[...]) + dot(matrix[:, 2 * POINTS :], yb[0:POINTS])

    def filter_and_mix(c):
        slot, hslot = lax.rem(c, 2), lax.rem(c, 3)
        own = gated[c]
        ghat[slot] = dot(f0[:, TAPS:], own) + dot(f1[:, TAPS:], own)

        @pl.when(has_previous)
        def _():
            gated_halo(c).wait_recv()

        @pl.when(me == 0)
        def _():
            g_halo[c] = jnp.zeros((TAPS, L), BF16)

        twice[0:TAPS] = g_halo[c]
        twice[TAPS:] = g_halo[c]
        ghat[slot] = ghat[slot] + dot(f2[...], twice[...])
        products(ghat.at[slot], hhat.at[hslot], False)
        mixed[slot] = back(f5)

    def multiply_cotangent(c):
        slot = lax.rem(c, 2)
        cot_own(c).wait()
        for k in (2, 1, 3):
            cot_wait(c, k)

        @pl.loop(0, TOK // 16, unroll=2)
        def _(r):
            rows = pl.ds(pl.multiple_of(r * 16, 16), 16)
            up = cot[c, rows].astype(F32)
            dm[c, rows] = (up * qs[c, rows]).astype(BF16)
            ds[c, 0, rows] = (up * mixed[slot, rows]).astype(BF16)

        @pl.when(has_previous)
        def _():
            mixed_halo(c).start()

    def filter_gradient(c):
        slot = lax.rem(c, 2)
        own = dm[c]
        dhat[slot] = dot(f0[:, :TOK], own) + dot(f1[:, :TOK], own)
        products(ghat.at[slot], dhat.at[slot], True)
        parts[c] = back(f7)

        @pl.loop(1, GROUP)
        def _(k):
            peer = lax.rem(g + k, GROUP)
            pltpu.make_async_remote_copy(
                src_ref=parts.at[c, pl.ds(pl.multiple_of(peer * 8, 8), 8)], dst_ref=landed.at[c, k - 1],
                send_sem=rs_sem.at[0, c], recv_sem=rs_sem.at[1, c], **to_seq(plane + peer)).start()

    def gated_gradient(c):
        slot, hslot = lax.rem(c, 2), lax.rem(c, 3)
        @pl.when(has_next)
        def _():
            mixed_halo(c).wait_recv()

        @pl.when(me == PEERS - 1)
        def _():
            dm_halo[c] = jnp.zeros((TAPS, L), BF16)

        twice[0:TAPS] = dm_halo[c]
        twice[TAPS:] = dm_halo[c]
        dhat[slot] = dhat[slot] + dot(f3[...], twice[...])
        products(dhat.at[slot], hhat.at[hslot], True)
        grad = back(f6)
        ds[c, 1, 0:TOK] = (grad * vs[c]).astype(BF16)
        ds[c, 2, 0:TOK] = (grad * ks[c]).astype(BF16)
        d_store(c).start()

        @pl.when(has_previous)
        def _():
            grad_halo(c).start()

    mine = pl.ds(pl.multiple_of(g * 8, 8), 8)

    def cross(c):
        return pltpu.make_async_remote_copy(
            src_ref=xs.at[c], dst_ref=xr.at[c], send_sem=xx_sem.at[0, c], recv_sem=xx_sem.at[1, c], **to_seq(across))

    def sum_plane(c):
        pltpu.make_async_copy(landed.at[c], landed.at[c], rs_sem.at[1, c]).wait()
        total = parts[c, mine]
        for k in range(GROUP - 1):
            total = total + landed[c, k]
        xs[c] = total
        cross(c).start()

    def spread(c):
        cross(c).wait_recv()
        sums[c, mine] = (xs[c] + xr[c]) * (1.0 / 128.0)

        @pl.loop(1, GROUP)
        def _(k):
            pltpu.make_async_remote_copy(
                src_ref=sums.at[c, mine], dst_ref=sums.at[c, mine],
                send_sem=ag_sem.at[0, c], recv_sem=ag_sem.at[1, c], **to_seq(mate(k))).start()

    def short_gradient(c):
        @pl.when(has_next)
        def _():
            grad_halo(c).wait_recv()

        @pl.when(me == PEERS - 1)
        def _():
            d_halo[c] = jnp.zeros((3, 16, L), BF16)

        halo_store(c).start()
        ds[c, :, TOK : TOK + 16] = d_halo[c]

        @pl.loop(0, 3 * LT)
        def _(n):
            i, l = n // LT, lax.rem(n, LT)
            cols = pl.ds(pl.multiple_of(l * 128, 128), 128)
            line[i] = ds[c, i, :, cols].astype(F32)

            def rows(b, acc):
                p = px[c, i, pl.ds(pl.multiple_of(16 + b * 64, 16), 64), cols].astype(F32)
                return tuple(
                    acc[j] + jnp.sum((line[i, pl.ds(b * 64 + j, 64)] * p).reshape(8, 8, 128), axis=0)
                    for j in range(SHORT))

            acc = lax.fori_loop(0, TOK // 64, rows, tuple(jnp.zeros((8, 128), F32) for _ in range(SHORT)), unroll=8)
            for j in range(SHORT):
                gs[c * LT + l, pl.ds(3 * i + j, 1)] = jnp.sum(acc[j], axis=0, keepdims=True)

        @pl.loop(0, 2 * LT)
        def _(n):
            owner = c * LT + lax.rem(n, LT)
            peer = owner + GROUP * (n // LT)

            @pl.when(peer != me)
            def _():
                pltpu.make_async_remote_copy(
                    src_ref=gs.at[owner], dst_ref=gs_landed.at[me],
                    send_sem=tail_sem.at[0], recv_sem=tail_sem.at[1], **to_seq(peer)).start()

    gs[...] = jnp.zeros(gs.shape, F32)
    filter_and_mix(0)

    @pl.loop(0, PARTS + 2)
    def _(s):
        @pl.when(s < PARTS)
        def _():
            multiply_cotangent(s)

        @pl.when(s + 2 < PARTS)
        def _():
            @pl.when(has_next)
            def _():
                gated_halo(s + 2).start()

            cot_start(s + 2)

        @pl.when(s < PARTS)
        def _():
            filter_gradient(s)

        @pl.when(s + 1 < PARTS)
        def _():
            filter_transform(s + 1)
            filter_and_mix(s + 1)

        @pl.when(jnp.logical_and(s >= 2, s <= PARTS))
        def _():
            sum_plane(s - 2)

        @pl.when(jnp.logical_and(s >= 1, s <= PARTS))
        def _():
            gated_gradient(s - 1)

        @pl.when(jnp.logical_and(s >= 2, s <= PARTS))
        def _():
            spread(s - 2)

        @pl.when(s == PARTS)
        def _():
            sum_plane(PARTS - 1)

        @pl.when(s == PARTS + 1)
        def _():
            spread(PARTS - 1)

        @pl.when(s >= 2)
        def _():
            short_gradient(s - 2)

    gs_landed[me] = gs[g]
    others = gs_landed.at[0 : PEERS - 1]
    mates = gs_landed.at[0 : GROUP - 1]
    pltpu.make_async_copy(others, others, tail_sem.at[1]).wait()
    total = gs_landed[0]
    for k in range(1, PEERS):
        total = total + gs_landed[k]
    gs_sums[g] = total * (1.0 / 128.0)

    @pl.loop(1, GROUP)
    def _(k):
        pltpu.make_async_remote_copy(
            src_ref=gs_sums.at[g], dst_ref=gs_sums.at[g],
            send_sem=tail_sem.at[2], recv_sem=tail_sem.at[3], **to_seq(mate(k))).start()

    def gl_store(c):
        return pltpu.make_async_copy(sums.at[c], gl_out.at[:, lanes(c)], h_sem.at[c])

    @pl.loop(0, PARTS)
    def _(c):
        pltpu.make_async_copy(landed.at[c], landed.at[c], ag_sem.at[1, c]).wait()
        gl_store(c).start()
        for k in (2, 1, 3):
            cot_send(c, k).wait_send()

        @pl.when(has_next)
        def _():
            p_halo(c).wait_send()
            gated_halo(c).wait_send()

        @pl.when(has_previous)
        def _():
            mixed_halo(c).wait_send()
            grad_halo(c).wait_send()

        cross(c).wait_send()
        pltpu.make_async_copy(landed.at[c], landed.at[c], rs_sem.at[0, c]).wait()
        pltpu.make_async_copy(landed.at[c], landed.at[c], ag_sem.at[0, c]).wait()
        d_store(c).wait()
        halo_store(c).wait()
        gl_store(c).wait()

    pltpu.make_async_copy(others, others, tail_sem.at[0]).wait()
    pltpu.make_async_copy(mates, mates, tail_sem.at[3]).wait()
    pltpu.make_async_copy(mates, mates, tail_sem.at[2]).wait()
    gs_out[...] = gs_sums[...]


ROWS = 256


def finish_kernel(sf_ref, d_ref, more_ref, gl_ref, gs_ref, gi_out, gl_out, skip_out, gs_out, line):
    i, b = pl.program_id(0), pl.program_id(1)

    @pl.loop(0, CH // 512)
    def _(quarter):
        for k in range(4):
            cols = pl.ds(pl.multiple_of(quarter * 512 + k * 128, 128), 128)
            line[k, 0:ROWS] = d_ref[0, :, cols].astype(F32)
            line[k, ROWS:] = more_ref[0, :, cols].astype(F32)
        for k in range(4):
            cols = pl.ds(pl.multiple_of(quarter * 512 + k * 128, 128), 128)
            taps = [sf_ref[i, j : j + 1, cols] for j in range(SHORT)]

            @pl.loop(0, ROWS // 64, unroll=4)
            def _(r):
                result = taps[0] * line[k, pl.ds(r * 64, 64)]
                for j in range(1, SHORT):
                    result = result + taps[j] * line[k, pl.ds(r * 64 + j, 64)]
                gi_out[0, pl.ds(pl.multiple_of(r * 64, 64), 64), cols] = result.astype(BF16)

    @pl.when(i == 0)
    def _():
        gl_out[...] = gl_ref[...]

    @pl.when(jnp.logical_and(i == 0, b == 0))
    def _():
        skip_out[...] = gl_ref[0]
        for stream in range(3):
            for j in range(SHORT):
                row = 3 * stream + j
                gs_out[stream, j : j + 1] = jnp.concatenate(
                    [gs_ref[t, row : row + 1] for t in range(GROUP)], axis=1)


def finish(short_filters, d, gl, gs):
    whole = lambda shape: pl.BlockSpec(shape, lambda i, b: (0,) * len(shape))
    steps = TOK // ROWS
    turn = pl.BlockSpec((TAPS // steps, CH), lambda i, b: (jnp.where(i == 0, b, steps - 1), 0))
    return pl.pallas_call(
        finish_kernel,
        grid=(3, steps),
        out_shape=(
            jax.ShapeDtypeStruct((3, TOK, CH), BF16),
            jax.ShapeDtypeStruct((TAPS, CH), F32),
            jax.ShapeDtypeStruct((CH,), F32),
            jax.ShapeDtypeStruct((3, SHORT, CH), F32),
        ),
        in_specs=[
            whole((3, SHORT, CH)),
            pl.BlockSpec((1, ROWS, CH), lambda i, b: (i, b, 0)),
            pl.BlockSpec((1, 16, CH), lambda i, b: (i, (b + 1) * (ROWS // 16), 0)),
            turn,
            whole((GROUP, 16, 128)),
        ],
        out_specs=(
            pl.BlockSpec((1, ROWS, CH), lambda i, b: (i, b, 0)),
            turn,
            whole((CH,)),
            whole((3, SHORT, CH)),
        ),
        scratch_shapes=[pltpu.VMEM((4, ROWS + 16, 128), F32)],
        compiler_params=pltpu.CompilerParams(vmem_limit_bytes=60 << 20),
        cost_estimate=pl.CostEstimate(flops=2 * 10**7, bytes_accessed=16 * 10**6, transcendentals=0),
    )(short_filters, d, d, gl, gs)


def per_device(projected, short_filters, long_filter, skip_gain, cotangent):
    mats = [jnp.asarray(m) for m in matrices()]
    anywhere = pl.BlockSpec(memory_space=pl.ANY)
    vmem = pl.BlockSpec(memory_space=pltpu.VMEM)
    dma = pltpu.SemaphoreType.DMA
    scratch = [
        pltpu.VMEM((PARTS, 3, TOK + 16, L), BF16),
        pltpu.VMEM((PARTS, 16, L), BF16),
        pltpu.VMEM((PARTS, 16, L), BF16),
        pltpu.VMEM((PARTS, TOK, L), F32),
        pltpu.VMEM((PARTS, TOK, L), F32),
        pltpu.VMEM((PARTS, TOK, L), F32),
        pltpu.VMEM((PARTS, TOK, L), BF16),
        pltpu.VMEM((PARTS, TAPS, L), BF16),
        pltpu.VMEM((2, POINTS, L), F32),
        pltpu.VMEM((3, POINTS, L), F32),
        pltpu.VMEM((2, TOK, L), F32),
        pltpu.VMEM((PARTS, TOK, L), BF16),
        pltpu.VMEM((PARTS, TOK, L), BF16),
        pltpu.VMEM((PARTS, TAPS, L), BF16),
        pltpu.VMEM((2, POINTS, L), F32),
        pltpu.VMEM((PARTS, 3, TOK + 16, L), BF16),
        pltpu.VMEM((PARTS, 3, 16, L), BF16),
        pltpu.VMEM((2 * POINTS, L), BF16),
        pltpu.VMEM((3 * TAPS, L), BF16),
        pltpu.VMEM((2 * TAPS, L), BF16),
        pltpu.VMEM((3, TOK + 16, 128), F32),
        pltpu.VMEM((PARTS, TAPS, L), F32),
        *[pltpu.VMEM(m.shape, BF16) for m in mats],
        pltpu.VMEM((PARTS, TAPS, L), F32),
        pltpu.VMEM((PARTS, GROUP - 1, 8, L), F32),
        pltpu.VMEM((PARTS, 8, L), F32),
        pltpu.VMEM((PARTS, 8, L), F32),
        pltpu.VMEM((PARTS, TAPS, L), F32),
        pltpu.VMEM((GROUP, 16, 128), F32),
        pltpu.VMEM((PEERS, 16, 128), F32),
        pltpu.VMEM((GROUP, 16, 128), F32),
        dma((PARTS,)),
        dma((len(mats),)),
        dma((PARTS,)),
        dma((PARTS,)),
        dma((PARTS,)),
        dma((PARTS,)),
        dma((PARTS, 3)),
        dma((PARTS, 3)),
        *[dma((2, PARTS)) for _ in range(7)],
        dma((4,)),
    ]
    d, gl, gs = pl.pallas_call(
        kernel,
        out_shape=(
            jax.ShapeDtypeStruct((3, TOK + 16, CH), BF16),
            jax.ShapeDtypeStruct((TAPS, CH), F32),
            jax.ShapeDtypeStruct((GROUP, 16, 128), F32),
        ),
        in_specs=[anywhere, vmem, anywhere, vmem, anywhere] + [anywhere] * len(mats),
        out_specs=(anywhere, anywhere, vmem),
        scratch_shapes=scratch,
        compiler_params=pltpu.CompilerParams(collective_id=0, has_side_effects=True, vmem_limit_bytes=62 << 20),
        cost_estimate=pl.CostEstimate(flops=20 * 10**9, bytes_accessed=24 * 10**6, transcendentals=0),
    )(projected, short_filters, long_filter, skip_gain[None], cotangent, *mats)
    return finish(short_filters, d, gl, gs)


def solution(mesh):
    placed = (
        P(None, "seq", "ch"),
        P(None, None, "ch"),
        P(None, "ch"),
        P("ch"),
        P(("seq", "ch"), None),
    )
    return jax.shard_map(
        per_device,
        mesh=mesh,
        in_specs=placed,
        out_specs=(P(None, "seq", "ch"), P(None, "ch"), P("ch"), P(None, None, "ch")),
        check_vma=False,
    )
```

```python
import functools

import jax
import jax.numpy as jnp
import numpy as np
from jax import lax
from jax.experimental import pallas as pl
from jax.experimental.pallas import tpu as pltpu
from jax.sharding import PartitionSpec as P

TAPS = 128
SHORT = 3
TOK = 512
CH = 2048
POINTS = TOK + TAPS
HALF = POINTS // 2
GROUP = 16
PEERS = 32
PARTS = 4
L = CH // PARTS
LT = L // 128
MESH = pl.DeviceIdType.MESH
F32, BF16 = jnp.float32, jnp.bfloat16


def split(x):
    high = x.astype(np.float32).astype(BF16)
    return high, (x - high.astype(np.float64)).astype(np.float32).astype(BF16)


@functools.cache
def matrices():
    angle = 2 * np.pi * np.outer(np.arange(HALF) + 0.5, np.arange(POINTS)) / POINTS
    forward = np.concatenate([np.cos(angle), -np.sin(angle)])
    inverse = (2.0 / POINTS) * np.concatenate([np.cos(angle.T), -np.sin(angle.T)], axis=1)
    fh, fl = split(forward)
    cat = lambda *parts: np.concatenate(parts, axis=1)
    first, last = slice(0, TAPS), slice(TOK, POINTS)

    def back(rows):
        high, low = split(inverse[rows])
        return cat(high, high, low)

    return (
        fh,
        fl,
        cat(fh[:, first], fl[:, first]),
        cat(fh[:, last], fl[:, last]),
        cat(fh[:, first], fl[:, first], fh[:, first]),
        back(np.arange(TAPS, POINTS)),
        back(np.arange(TOK)),
        back(TAPS - np.arange(TAPS)),
    )


def dot(a, b):
    return jnp.dot(a, b, preferred_element_type=F32)


def kernel(
    proj, sf_ref, h_hbm, skip_ref, cot_hbm, m0, m1, m2, m3, m4, m5, m6, m7,
    d_out, gl_out, gs_out,
    px, tip, p_halo_ref, qs, ks, vs, gated, g_halo, ghat, hhat, mixed, cot, dm, dm_halo, dhat, ds, d_halo,
    yb, hb, twice, line, hv, f0, f1, f2, f3, f4, f5, f6, f7,
    parts, landed, xs, xr, shared, sums, gs, gs_landed, gs_sums,
    load_sem, mat_sem, h_sem, own_sem, out_sem, halo_out_sem, a2a_send, a2a_recv,
    ph_sem, gh_sem, dmh_sem, dh_sem, rs_sem, xx_sem, ag_sem, tail_sem,
):
    me = lax.axis_index("seq")
    col = lax.axis_index("ch")
    g = lax.rem(me, GROUP)
    plane = me - g
    nxt, prv = lax.rem(me + 1, PEERS), lax.rem(me + PEERS - 1, PEERS)
    across = lax.rem(me + GROUP, PEERS)
    barrier = pltpu.get_barrier_semaphore()

    def to_seq(s):
        return dict(device_id={"seq": s}, device_id_type=MESH)

    def to_ch(c):
        return dict(device_id={"ch": c}, device_id_type=MESH)

    def mate(k):
        return plane + lax.rem(g + k, GROUP)

    def lanes(c):
        return pl.ds(pl.multiple_of(c * L, L), L)

    def p_load(c):
        return pltpu.make_async_copy(proj.at[:, :, lanes(c)], px.at[c, :, 16 : 16 + TOK], load_sem.at[c])

    def h_load(c):
        return pltpu.make_async_copy(h_hbm.at[:, lanes(c)], hv.at[c], h_sem.at[c])

    mats = [
        pltpu.make_async_copy(a, b, mat_sem.at[i])
        for i, (a, b) in enumerate(zip((m0, m1, m2, m3, m4, m5, m6, m7), (f0, f1, f2, f3, f4, f5, f6, f7)))
    ]
    p_load(0).start()
    p_load(1).start()

    @pl.loop(1, PEERS)
    def _(k):
        pl.semaphore_signal(barrier, inc=1, **to_seq(lax.rem(me + k, PEERS)))

    for k in range(1, 4):
        pl.semaphore_signal(barrier, inc=1, **to_ch(lax.rem(col + k, 4)))


    def cot_block(c, owner):
        return cot.at[c, pl.ds(pl.multiple_of(owner * 128, 128), 128)]

    def cot_own(c):
        cols = pl.ds(pl.multiple_of(col * CH + c * L, L), L)
        return pltpu.make_async_copy(cot_hbm.at[:, cols], cot_block(c, col), own_sem.at[c])

    def cot_send(c, k):
        peer = lax.rem(col + k, 4)
        cols = pl.ds(pl.multiple_of(peer * CH + c * L, L), L)
        return pltpu.make_async_remote_copy(
            src_ref=cot_hbm.at[:, cols], dst_ref=cot_block(c, col),
            send_sem=a2a_send.at[c, k - 1], recv_sem=a2a_recv.at[c, k - 1], **to_ch(peer))

    def cot_wait(c, k):
        block = cot_block(c, lax.rem(col + 4 - k, 4))
        pltpu.make_async_copy(block, block, a2a_recv.at[c, k - 1]).wait()

    def p_halo(c):
        return pltpu.make_async_remote_copy(
            src_ref=tip.at[c], dst_ref=p_halo_ref.at[c],
            send_sem=ph_sem.at[0, c], recv_sem=ph_sem.at[1, c], **to_seq(nxt))

    def gated_halo(c):
        return pltpu.make_async_remote_copy(
            src_ref=gated.at[c, TOK - TAPS : TOK], dst_ref=g_halo.at[c],
            send_sem=gh_sem.at[0, c], recv_sem=gh_sem.at[1, c], **to_seq(nxt))

    def mixed_halo(c):
        return pltpu.make_async_remote_copy(
            src_ref=dm.at[c, 0:TAPS], dst_ref=dm_halo.at[c],
            send_sem=dmh_sem.at[0, c], recv_sem=dmh_sem.at[1, c], **to_seq(prv))

    def grad_halo(c):
        return pltpu.make_async_remote_copy(
            src_ref=ds.at[c, :, 0:16], dst_ref=d_halo.at[c],
            send_sem=dh_sem.at[0, c], recv_sem=dh_sem.at[1, c], **to_seq(prv))

    def d_store(c):
        return pltpu.make_async_copy(ds.at[c, 0:2, 0:TOK], d_out.at[0:2, 0:TOK, lanes(c)], out_sem.at[0, c])

    def last_store(c):
        return pltpu.make_async_copy(ds.at[c, 2, 0:TOK], d_out.at[2, 0:TOK, lanes(c)], out_sem.at[1, c])

    def halo_store(c):
        return pltpu.make_async_copy(d_halo.at[c], d_out.at[:, TOK : TOK + 16, lanes(c)], halo_out_sem.at[c])

    def cot_start(c):
        cot_own(c).start()
        for k in (2, 1, 3):
            cot_send(c, k).start()

    has_next, has_previous = me < PEERS - 1, me > 0

    def stream_rows(c, l):
        cols = pl.ds(pl.multiple_of(l * 128, 128), 128)
        wide = pl.ds(pl.multiple_of(c * L + l * 128, 128), 128)
        for i in range(3):
            line[i] = px[c, i, :, cols].astype(F32)
        taps = [[sf_ref[i, j : j + 1, wide] for j in range(SHORT)] for i in range(3)]

        @pl.loop(0, TOK // 64, unroll=4)
        def _(b):
            here = pl.ds(pl.multiple_of(b * 64, 64), 64)
            out = []
            for i, keep in enumerate((qs, ks, vs)):
                s = taps[i][0] * line[i, pl.ds(b * 64 + 16, 64)]
                s = s + taps[i][1] * line[i, pl.ds(b * 64 + 15, 64)]
                s = s + taps[i][2] * line[i, pl.ds(b * 64 + 14, 64)]
                keep[c, here, cols] = s
                out.append(s)
            gated[c, here, cols] = (out[1] * out[2]).astype(BF16)

    pl.semaphore_wait(barrier, PEERS - 1 + 3)
    cot_start(0)

    @pl.loop(0, PARTS)
    def _(c):
        p_load(c).wait()

        @pl.when(c + 2 < PARTS)
        def _():
            p_load(c + 2).start()

        @pl.when(c == 0)
        def _():
            h_load(0).start()
            mats[4].start()

        @pl.when(c == 1)
        def _():
            for i in (0, 1, 2, 5, 7, 6, 3):
                mats[i].start()
            for k in range(1, PARTS):
                h_load(k).start()

        px[c, :, 0:16] = jnp.zeros((3, 16, L), BF16)
        last = [px[c, i, TOK : TOK + 16].astype(F32)[14:16] for i in range(3)]
        tip[c] = jnp.concatenate(last + [jnp.zeros((10, L), F32)], axis=0).astype(BF16)

        @pl.when(has_next)
        def _():
            p_halo(c).start()

        @pl.loop(0, LT)
        def _(l):
            stream_rows(c, l)

        @pl.when(jnp.logical_and(has_next, c == 0))
        def _():
            gated_halo(c).start()

    @pl.when(has_next)
    def _():
        gated_halo(1).start()

    cot_start(1)
    mats[4].wait()

    def filter_transform(c):
        h_load(c).wait()
        h = hv[c]
        high = h.astype(BF16)
        hb[0:TAPS] = high
        hb[TAPS : 2 * TAPS] = high
        hb[2 * TAPS :] = (h - high.astype(F32)).astype(BF16)
        hslot = lax.rem(c, 3)
        hhat[hslot] = dot(f4[...], hb[...])
        hhat[hslot, 0:HALF] = hhat[hslot, 0:HALF] + skip_ref[0:1, lanes(c)]

    filter_transform(0)

    @pl.loop(0, PARTS)
    def _(c):
        @pl.when(has_previous)
        def _():
            p_halo(c).wait_recv()

        @pl.when(me == 0)
        def _():
            p_halo_ref[c] = jnp.zeros((16, L), BF16)

        before = p_halo_ref[c].astype(F32)
        out = []
        for i, keep in enumerate((qs, ks, vs)):
            x = jnp.concatenate([before[2 * i : 2 * i + 2], px[c, i, 16:32].astype(F32)], axis=0)
            s = sf_ref[i, 0:1, lanes(c)] * x[2:18]
            s = s + sf_ref[i, 1:2, lanes(c)] * x[1:17]
            s = s + sf_ref[i, 2:3, lanes(c)] * x[0:16]
            keep[c, 0:16] = s
            out.append(s)
        gated[c, 0:16] = (out[1] * out[2]).astype(BF16)

    def products(a, b, conj):
        @pl.loop(0, HALF // 16, unroll=2)
        def _(r):
            rows = pl.ds(pl.multiple_of(r * 16, 16), 16)
            rows_i = pl.ds(pl.multiple_of(HALF + r * 16, 16), 16)
            ar, ai, br, bi = a[rows], a[rows_i], b[rows], b[rows_i]
            if conj:
                re, im = ar * br + ai * bi, ai * br - ar * bi
            else:
                re, im = ar * br - ai * bi, ar * bi + ai * br
            for value, start in ((re, 0), (im, HALF)):
                high = value.astype(BF16)
                at = pl.multiple_of(start + r * 16, 16)
                yb[pl.ds(at, 16)] = high
                yb[pl.ds(POINTS + at, 16)] = (value - high.astype(F32)).astype(BF16)

    def back(matrix):
        return dot(matrix[:, : 2 * POINTS], yb[...]) + dot(matrix[:, 2 * POINTS :], yb[0:POINTS])

    def filter_and_mix(c):
        slot, hslot = lax.rem(c, 2), lax.rem(c, 3)
        own = gated[c]
        ghat[slot] = dot(f0[:, TAPS:], own) + dot(f1[:, TAPS:], own)

        @pl.when(has_previous)
        def _():
            gated_halo(c).wait_recv()

        @pl.when(me == 0)
        def _():
            g_halo[c] = jnp.zeros((TAPS, L), BF16)

        twice[0:TAPS] = g_halo[c]
        twice[TAPS:] = g_halo[c]
        ghat[slot] = ghat[slot] + dot(f2[...], twice[...])
        products(ghat.at[slot], hhat.at[hslot], False)
        mixed[slot] = back(f5)

    def multiply_cotangent(c):
        slot = lax.rem(c, 2)
        cot_own(c).wait()
        for k in (2, 1, 3):
            cot_wait(c, k)

        @pl.loop(0, TOK // 16, unroll=2)
        def _(r):
            rows = pl.ds(pl.multiple_of(r * 16, 16), 16)
            up = cot[c, rows].astype(F32)
            dm[c, rows] = (up * qs[c, rows]).astype(BF16)
            ds[c, 0, rows] = (up * mixed[slot, rows]).astype(BF16)

        @pl.when(has_previous)
        def _():
            mixed_halo(c).start()

    def filter_gradient(c):
        slot = lax.rem(c, 2)
        own = dm[c]
        dhat[slot] = dot(f0[:, :TOK], own) + dot(f1[:, :TOK], own)
        products(ghat.at[slot], dhat.at[slot], True)
        parts[c] = back(f7)

        @pl.loop(1, GROUP)
        def _(k):
            peer = lax.rem(g + k, GROUP)
            pltpu.make_async_remote_copy(
                src_ref=parts.at[c, pl.ds(pl.multiple_of(peer * 8, 8), 8)], dst_ref=landed.at[c, k - 1],
                send_sem=rs_sem.at[0, c], recv_sem=rs_sem.at[1, c], **to_seq(plane + peer)).start()

    def gated_gradient(c):
        slot, hslot = lax.rem(c, 2), lax.rem(c, 3)
        @pl.when(has_next)
        def _():
            mixed_halo(c).wait_recv()

        @pl.when(me == PEERS - 1)
        def _():
            dm_halo[c] = jnp.zeros((TAPS, L), BF16)

        twice[0:TAPS] = dm_halo[c]
        twice[TAPS:] = dm_halo[c]
        dhat[slot] = dhat[slot] + dot(f3[...], twice[...])
        products(dhat.at[slot], hhat.at[hslot], True)
        grad = back(f6)
        ds[c, 1, 0:TOK] = (grad * vs[c]).astype(BF16)
        ds[c, 2, 0:TOK] = (grad * ks[c]).astype(BF16)
        d_store(c).start()

        @pl.when(has_previous)
        def _():
            grad_halo(c).start()

    mine = pl.ds(pl.multiple_of(g * 8, 8), 8)

    def cross(c):
        return pltpu.make_async_remote_copy(
            src_ref=xs.at[c], dst_ref=xr.at[c], send_sem=xx_sem.at[0, c], recv_sem=xx_sem.at[1, c], **to_seq(across))

    def sum_plane(c):
        pltpu.make_async_copy(landed.at[c], landed.at[c], rs_sem.at[1, c]).wait()
        total = parts[c, mine]
        for k in range(GROUP - 1):
            total = total + landed[c, k]
        xs[c] = total
        cross(c).start()

    def spread(c):
        cross(c).wait_recv()
        total = (xs[c] + xr[c]) * (1.0 / 128.0)
        shared[c, g] = jnp.concatenate([total[:, : L // 2], total[:, L // 2 :]], axis=0).astype(BF16)

        @pl.loop(1, GROUP)
        def _(k):
            pltpu.make_async_remote_copy(
                src_ref=shared.at[c, g], dst_ref=shared.at[c, g],
                send_sem=ag_sem.at[0, c], recv_sem=ag_sem.at[1, c], **to_seq(mate(k))).start()

    def short_gradient(c):
        @pl.when(has_next)
        def _():
            grad_halo(c).wait_recv()

        @pl.when(me == PEERS - 1)
        def _():
            d_halo[c] = jnp.zeros((3, 16, L), BF16)

        halo_store(c).start()
        ds[c, :, TOK : TOK + 16] = d_halo[c]

        @pl.loop(0, 3 * LT)
        def _(n):
            i, l = n // LT, lax.rem(n, LT)
            cols = pl.ds(pl.multiple_of(l * 128, 128), 128)
            line[i] = ds[c, i, :, cols].astype(F32)

            def rows(b, acc):
                p = px[c, i, pl.ds(pl.multiple_of(16 + b * 64, 16), 64), cols].astype(F32)
                return tuple(
                    acc[j] + jnp.sum((line[i, pl.ds(b * 64 + j, 64)] * p).reshape(8, 8, 128), axis=0)
                    for j in range(SHORT))

            acc = lax.fori_loop(0, TOK // 64, rows, tuple(jnp.zeros((8, 128), F32) for _ in range(SHORT)), unroll=8)
            for j in range(SHORT):
                gs[c * LT + l, pl.ds(3 * i + j, 1)] = jnp.sum(acc[j], axis=0, keepdims=True)

        @pl.loop(0, 2 * LT)
        def _(n):
            owner = c * LT + lax.rem(n, LT)
            peer = owner + GROUP * (n // LT)

            @pl.when(peer != me)
            def _():
                pltpu.make_async_remote_copy(
                    src_ref=gs.at[owner], dst_ref=gs_landed.at[me],
                    send_sem=tail_sem.at[0], recv_sem=tail_sem.at[1], **to_seq(peer)).start()

    gs[...] = jnp.zeros(gs.shape, F32)
    for i in (0, 1, 2, 5):
        mats[i].wait()
    filter_and_mix(0)
    for i in (7, 6, 3):
        mats[i].wait()

    @pl.loop(0, PARTS + 2)
    def _(s):
        @pl.when(s < PARTS)
        def _():
            multiply_cotangent(s)

        @pl.when(s + 2 < PARTS)
        def _():
            @pl.when(has_next)
            def _():
                gated_halo(s + 2).start()

            cot_start(s + 2)

        @pl.when(s < PARTS)
        def _():
            filter_gradient(s)

        @pl.when(s + 1 < PARTS)
        def _():
            filter_transform(s + 1)
            filter_and_mix(s + 1)

        @pl.when(jnp.logical_and(s >= 2, s <= PARTS))
        def _():
            sum_plane(s - 2)

        @pl.when(jnp.logical_and(s >= 1, s <= PARTS))
        def _():
            gated_gradient(s - 1)

        @pl.when(jnp.logical_and(s >= 2, s <= PARTS))
        def _():
            spread(s - 2)

        @pl.when(s == PARTS)
        def _():
            sum_plane(PARTS - 1)

        @pl.when(s == PARTS + 1)
        def _():
            spread(PARTS - 1)

        @pl.when(s >= 2)
        def _():
            short_gradient(s - 2)

    @pl.loop(0, PARTS)
    def _(c):
        @pl.when(has_previous)
        def _():
            grad_halo(c).wait_send()

        @pl.loop(0, LT)
        def _(l):
            cols = pl.ds(pl.multiple_of(l * 128, 128), 128)
            wide = pl.ds(pl.multiple_of(c * L + l * 128, 128), 128)
            line[0] = ds[c, 2, :, cols].astype(F32)
            taps = [sf_ref[2, j : j + 1, wide] for j in range(SHORT)]

            @pl.loop(0, TOK // 64, unroll=4)
            def _(r):
                result = taps[0] * line[0, pl.ds(r * 64, 64)]
                for j in range(1, SHORT):
                    result = result + taps[j] * line[0, pl.ds(r * 64 + j, 64)]
                ds[c, 2, pl.ds(pl.multiple_of(r * 64, 64), 64), cols] = result.astype(BF16)

        last_store(c).start()

    gs_landed[me] = gs[g]
    others = gs_landed.at[0 : PEERS - 1]
    mates = gs_landed.at[0 : GROUP - 1]
    pltpu.make_async_copy(others, others, tail_sem.at[1]).wait()
    total = gs_landed[0]
    for k in range(1, PEERS):
        total = total + gs_landed[k]
    gs_sums[g] = total * (1.0 / 128.0)

    @pl.loop(1, GROUP)
    def _(k):
        pltpu.make_async_remote_copy(
            src_ref=gs_sums.at[g], dst_ref=gs_sums.at[g],
            send_sem=tail_sem.at[2], recv_sem=tail_sem.at[3], **to_seq(mate(k))).start()

    def gl_store(c):
        return pltpu.make_async_copy(sums.at[c], gl_out.at[:, lanes(c)], h_sem.at[c])

    @pl.loop(0, PARTS)
    def _(c):
        fifteen = shared.at[c, 0 : GROUP - 1]
        pltpu.make_async_copy(fifteen, fifteen, ag_sem.at[1, c]).wait()
        for p in range(GROUP):
            piece = shared[c, p].astype(F32)
            sums[c, 8 * p : 8 * p + 8, : L // 2] = piece[0:8]
            sums[c, 8 * p : 8 * p + 8, L // 2 :] = piece[8:16]
        gl_store(c).start()
        for k in (2, 1, 3):
            cot_send(c, k).wait_send()

        @pl.when(has_next)
        def _():
            p_halo(c).wait_send()
            gated_halo(c).wait_send()

        @pl.when(has_previous)
        def _():
            mixed_halo(c).wait_send()

        cross(c).wait_send()
        pltpu.make_async_copy(landed.at[c], landed.at[c], rs_sem.at[0, c]).wait()
        pltpu.make_async_copy(fifteen, fifteen, ag_sem.at[0, c]).wait()
        d_store(c).wait()
        last_store(c).wait()
        halo_store(c).wait()
        gl_store(c).wait()

    pltpu.make_async_copy(others, others, tail_sem.at[0]).wait()
    pltpu.make_async_copy(mates, mates, tail_sem.at[3]).wait()
    pltpu.make_async_copy(mates, mates, tail_sem.at[2]).wait()
    gs_out[...] = gs_sums[...]


ROWS = 256


def finish_kernel(sf_ref, d_ref, more_ref, gl_ref, gs_ref, gi_out, gl_out, skip_out, gs_out, line):
    i, b = pl.program_id(0), pl.program_id(1)

    @pl.when(i < 2)
    def _():
        @pl.loop(0, CH // 512)
        def _(quarter):
            for k in range(4):
                cols = pl.ds(pl.multiple_of(quarter * 512 + k * 128, 128), 128)
                line[k, 0:ROWS] = d_ref[0, :, cols].astype(F32)
                line[k, ROWS:] = more_ref[0, :, cols].astype(F32)
            for k in range(4):
                cols = pl.ds(pl.multiple_of(quarter * 512 + k * 128, 128), 128)
                taps = [sf_ref[i, j : j + 1, cols] for j in range(SHORT)]

                @pl.loop(0, ROWS // 64, unroll=4)
                def _(r):
                    result = taps[0] * line[k, pl.ds(r * 64, 64)]
                    for j in range(1, SHORT):
                        result = result + taps[j] * line[k, pl.ds(r * 64 + j, 64)]
                    gi_out[0, pl.ds(pl.multiple_of(r * 64, 64), 64), cols] = result.astype(BF16)

    @pl.when(i == 2)
    def _():
        gi_out[...] = d_ref[...]

    @pl.when(i == 0)
    def _():
        gl_out[...] = gl_ref[...]

    @pl.when(jnp.logical_and(i == 0, b == 0))
    def _():
        skip_out[...] = gl_ref[0]
        for stream in range(3):
            for j in range(SHORT):
                row = 3 * stream + j
                gs_out[stream, j : j + 1] = jnp.concatenate(
                    [gs_ref[t, row : row + 1] for t in range(GROUP)], axis=1)


def finish(short_filters, d, gl, gs):
    whole = lambda shape: pl.BlockSpec(shape, lambda i, b: (0,) * len(shape))
    steps = TOK // ROWS
    turn = pl.BlockSpec((TAPS // steps, CH), lambda i, b: (jnp.where(i == 0, b, steps - 1), 0))
    return pl.pallas_call(
        finish_kernel,
        grid=(3, steps),
        out_shape=(
            jax.ShapeDtypeStruct((3, TOK, CH), BF16),
            jax.ShapeDtypeStruct((TAPS, CH), F32),
            jax.ShapeDtypeStruct((CH,), F32),
            jax.ShapeDtypeStruct((3, SHORT, CH), F32),
        ),
        in_specs=[
            whole((3, SHORT, CH)),
            pl.BlockSpec((1, ROWS, CH), lambda i, b: (i, b, 0)),
            pl.BlockSpec((1, 16, CH), lambda i, b: (i, (b + 1) * (ROWS // 16), 0)),
            turn,
            whole((GROUP, 16, 128)),
        ],
        out_specs=(
            pl.BlockSpec((1, ROWS, CH), lambda i, b: (i, b, 0)),
            turn,
            whole((CH,)),
            whole((3, SHORT, CH)),
        ),
        scratch_shapes=[pltpu.VMEM((4, ROWS + 16, 128), F32)],
        compiler_params=pltpu.CompilerParams(vmem_limit_bytes=60 << 20),
        cost_estimate=pl.CostEstimate(flops=2 * 10**7, bytes_accessed=16 * 10**6, transcendentals=0),
    )(short_filters, d, d, gl, gs)


def per_device(projected, short_filters, long_filter, skip_gain, cotangent):
    mats = [jnp.asarray(m) for m in matrices()]
    anywhere = pl.BlockSpec(memory_space=pl.ANY)
    vmem = pl.BlockSpec(memory_space=pltpu.VMEM)
    dma = pltpu.SemaphoreType.DMA
    scratch = [
        pltpu.VMEM((PARTS, 3, TOK + 16, L), BF16),
        pltpu.VMEM((PARTS, 16, L), BF16),
        pltpu.VMEM((PARTS, 16, L), BF16),
        pltpu.VMEM((PARTS, TOK, L), F32),
        pltpu.VMEM((PARTS, TOK, L), F32),
        pltpu.VMEM((PARTS, TOK, L), F32),
        pltpu.VMEM((PARTS, TOK, L), BF16),
        pltpu.VMEM((PARTS, TAPS, L), BF16),
        pltpu.VMEM((2, POINTS, L), F32),
        pltpu.VMEM((3, POINTS, L), F32),
        pltpu.VMEM((2, TOK, L), F32),
        pltpu.VMEM((PARTS, TOK, L), BF16),
        pltpu.VMEM((PARTS, TOK, L), BF16),
        pltpu.VMEM((PARTS, TAPS, L), BF16),
        pltpu.VMEM((2, POINTS, L), F32),
        pltpu.VMEM((PARTS, 3, TOK + 16, L), BF16),
        pltpu.VMEM((PARTS, 3, 16, L), BF16),
        pltpu.VMEM((2 * POINTS, L), BF16),
        pltpu.VMEM((3 * TAPS, L), BF16),
        pltpu.VMEM((2 * TAPS, L), BF16),
        pltpu.VMEM((3, TOK + 16, 128), F32),
        pltpu.VMEM((PARTS, TAPS, L), F32),
        *[pltpu.VMEM(m.shape, BF16) for m in mats],
        pltpu.VMEM((PARTS, TAPS, L), F32),
        pltpu.VMEM((PARTS, GROUP - 1, 8, L), F32),
        pltpu.VMEM((PARTS, 8, L), F32),
        pltpu.VMEM((PARTS, 8, L), F32),
        pltpu.VMEM((PARTS, GROUP, 16, L // 2), BF16),
        pltpu.VMEM((PARTS, TAPS, L), F32),
        pltpu.VMEM((GROUP, 16, 128), F32),
        pltpu.VMEM((PEERS, 16, 128), F32),
        pltpu.VMEM((GROUP, 16, 128), F32),
        dma((PARTS,)),
        dma((len(mats),)),
        dma((PARTS,)),
        dma((PARTS,)),
        dma((2, PARTS)),
        dma((PARTS,)),
        dma((PARTS, 3)),
        dma((PARTS, 3)),
        *[dma((2, PARTS)) for _ in range(7)],
        dma((4,)),
    ]
    d, gl, gs = pl.pallas_call(
        kernel,
        out_shape=(
            jax.ShapeDtypeStruct((3, TOK + 16, CH), BF16),
            jax.ShapeDtypeStruct((TAPS, CH), F32),
            jax.ShapeDtypeStruct((GROUP, 16, 128), F32),
        ),
        in_specs=[anywhere, vmem, anywhere, vmem, anywhere] + [anywhere] * len(mats),
        out_specs=(anywhere, anywhere, vmem),
        scratch_shapes=scratch,
        compiler_params=pltpu.CompilerParams(collective_id=0, has_side_effects=True, vmem_limit_bytes=62 << 20),
        cost_estimate=pl.CostEstimate(flops=20 * 10**9, bytes_accessed=24 * 10**6, transcendentals=0),
    )(projected, short_filters, long_filter, skip_gain[None], cotangent, *mats)
    return finish(short_filters, d, gl, gs)


def solution(mesh):
    placed = (
        P(None, "seq", "ch"),
        P(None, None, "ch"),
        P(None, "ch"),
        P("ch"),
        P(("seq", "ch"), None),
    )
    return jax.shard_map(
        per_device,
        mesh=mesh,
        in_specs=placed,
        out_specs=(P(None, "seq", "ch"), P(None, "ch"), P("ch"), P(None, None, "ch")),
        check_vma=False,
    )
```

```python
import functools

import jax
import jax.numpy as jnp
import numpy as np
from jax import lax
from jax.experimental import pallas as pl
from jax.experimental.pallas import tpu as pltpu
from jax.sharding import PartitionSpec as P

TAPS = 128
SHORT = 3
TOK = 512
CH = 2048
POINTS = TOK + TAPS
HALF = POINTS // 2
GROUP = 16
PEERS = 32
PARTS = 4
L = CH // PARTS
LT = L // 128
MESH = pl.DeviceIdType.MESH
F32, BF16 = jnp.float32, jnp.bfloat16


def split(x):
    high = x.astype(np.float32).astype(BF16)
    return high, (x - high.astype(np.float64)).astype(np.float32).astype(BF16)


@functools.cache
def matrices():
    angle = 2 * np.pi * np.outer(np.arange(HALF) + 0.5, np.arange(POINTS)) / POINTS
    forward = np.concatenate([np.cos(angle), -np.sin(angle)])
    inverse = (2.0 / POINTS) * np.concatenate([np.cos(angle.T), -np.sin(angle.T)], axis=1)
    fh, fl = split(forward)
    cat = lambda *parts: np.concatenate(parts, axis=1)
    first, last = slice(0, TAPS), slice(TOK, POINTS)

    def back(rows):
        high, low = split(inverse[rows])
        return cat(high, high, low)

    return (
        fh,
        fl,
        cat(fh[:, first], fl[:, first]),
        cat(fh[:, last], fl[:, last]),
        cat(fh[:, first], fl[:, first], fh[:, first]),
        back(np.arange(TAPS, POINTS)),
        back(np.arange(TOK)),
        back(TAPS - np.arange(TAPS)),
    )


def dot(a, b):
    return jnp.dot(a, b, preferred_element_type=F32)


def kernel(
    proj, sf_ref, h_hbm, skip_ref, cot_hbm, m0, m1, m2, m3, m4, m5, m6, m7,
    d_out, gl_out, gs_out,
    px, tip, p_halo_ref, qs, ks, vs, gated, g_halo, ghat, hhat, mixed, cot, dm, dm_halo, dhat, ds, d_halo,
    yb, hb, twice, line, hv, f0, f1, f2, f3, f4, f5, f6, f7,
    parts, landed, xs, xr, shared, sums, gs, gs_landed, gs_sums,
    load_sem, mat_sem, h_sem, own_sem, out_sem, halo_out_sem, a2a_send, a2a_recv,
    ph_sem, gh_sem, dmh_sem, dh_sem, rs_sem, xx_sem, ag_sem, tail_sem,
):
    me = lax.axis_index("seq")
    col = lax.axis_index("ch")
    g = lax.rem(me, GROUP)
    plane = me - g
    nxt, prv = lax.rem(me + 1, PEERS), lax.rem(me + PEERS - 1, PEERS)
    across = lax.rem(me + GROUP, PEERS)
    barrier = pltpu.get_barrier_semaphore()

    def to_seq(s):
        return dict(device_id={"seq": s}, device_id_type=MESH)

    def to_ch(c):
        return dict(device_id={"ch": c}, device_id_type=MESH)

    def mate(k):
        return plane + lax.rem(g + k, GROUP)

    def lanes(c):
        return pl.ds(pl.multiple_of(c * L, L), L)

    def p_load(c):
        return pltpu.make_async_copy(proj.at[:, :, lanes(c)], px.at[c, :, 16 : 16 + TOK], load_sem.at[c])

    def h_load(c):
        return pltpu.make_async_copy(h_hbm.at[:, lanes(c)], hv.at[c], h_sem.at[c])

    mats = [
        pltpu.make_async_copy(a, b, mat_sem.at[i])
        for i, (a, b) in enumerate(zip((m0, m1, m2, m3, m4, m5, m6, m7), (f0, f1, f2, f3, f4, f5, f6, f7)))
    ]
    p_load(0).start()
    p_load(1).start()

    @pl.loop(1, PEERS)
    def _(k):
        pl.semaphore_signal(barrier, inc=1, **to_seq(lax.rem(me + k, PEERS)))

    for k in range(1, 4):
        pl.semaphore_signal(barrier, inc=1, **to_ch(lax.rem(col + k, 4)))


    def cot_block(c, owner):
        return cot.at[c, pl.ds(pl.multiple_of(owner * 128, 128), 128)]

    def cot_own(c):
        cols = pl.ds(pl.multiple_of(col * CH + c * L, L), L)
        return pltpu.make_async_copy(cot_hbm.at[:, cols], cot_block(c, col), own_sem.at[c])

    def cot_send(c, k):
        peer = lax.rem(col + k, 4)
        cols = pl.ds(pl.multiple_of(peer * CH + c * L, L), L)
        return pltpu.make_async_remote_copy(
            src_ref=cot_hbm.at[:, cols], dst_ref=cot_block(c, col),
            send_sem=a2a_send.at[c, k - 1], recv_sem=a2a_recv.at[c, k - 1], **to_ch(peer))

    def cot_wait(c, k):
        block = cot_block(c, lax.rem(col + 4 - k, 4))
        pltpu.make_async_copy(block, block, a2a_recv.at[c, k - 1]).wait()

    def p_halo(c):
        return pltpu.make_async_remote_copy(
            src_ref=tip.at[c], dst_ref=p_halo_ref.at[c],
            send_sem=ph_sem.at[0, c], recv_sem=ph_sem.at[1, c], **to_seq(nxt))

    def gated_halo(c):
        return pltpu.make_async_remote_copy(
            src_ref=gated.at[c, TOK - TAPS : TOK], dst_ref=g_halo.at[c],
            send_sem=gh_sem.at[0, c], recv_sem=gh_sem.at[1, c], **to_seq(nxt))

    def mixed_halo(c):
        return pltpu.make_async_remote_copy(
            src_ref=dm.at[c, 0:TAPS], dst_ref=dm_halo.at[c],
            send_sem=dmh_sem.at[0, c], recv_sem=dmh_sem.at[1, c], **to_seq(prv))

    def grad_halo(c):
        return pltpu.make_async_remote_copy(
            src_ref=ds.at[c, :, 0:16], dst_ref=d_halo.at[c],
            send_sem=dh_sem.at[0, c], recv_sem=dh_sem.at[1, c], **to_seq(prv))

    def d_store(i, c):
        return pltpu.make_async_copy(ds.at[c, i, 0:TOK], d_out.at[i, 0:TOK, lanes(c)], out_sem.at[i, c])

    def halo_store(c):
        return pltpu.make_async_copy(d_halo.at[c], d_out.at[:, TOK : TOK + 16, lanes(c)], halo_out_sem.at[c])

    def cot_start(c):
        cot_own(c).start()
        for k in (2, 1, 3):
            cot_send(c, k).start()

    has_next, has_previous = me < PEERS - 1, me > 0

    def stream_rows(c, l):
        cols = pl.ds(pl.multiple_of(l * 128, 128), 128)
        wide = pl.ds(pl.multiple_of(c * L + l * 128, 128), 128)
        for i in range(3):
            line[i] = px[c, i, :, cols].astype(F32)
        taps = [[sf_ref[i, j : j + 1, wide] for j in range(SHORT)] for i in range(3)]

        @pl.loop(0, TOK // 64, unroll=4)
        def _(b):
            here = pl.ds(pl.multiple_of(b * 64, 64), 64)
            out = []
            for i, keep in enumerate((qs, ks, vs)):
                s = taps[i][0] * line[i, pl.ds(b * 64 + 16, 64)]
                s = s + taps[i][1] * line[i, pl.ds(b * 64 + 15, 64)]
                s = s + taps[i][2] * line[i, pl.ds(b * 64 + 14, 64)]
                keep[c, here, cols] = s
                out.append(s)
            gated[c, here, cols] = (out[1] * out[2]).astype(BF16)

    pl.semaphore_wait(barrier, PEERS - 1 + 3)
    cot_start(0)

    @pl.loop(0, PARTS)
    def _(c):
        p_load(c).wait()

        @pl.when(c + 2 < PARTS)
        def _():
            p_load(c + 2).start()

        @pl.when(c == 0)
        def _():
            h_load(0).start()
            mats[4].start()

        @pl.when(c == 1)
        def _():
            for i in (0, 1, 2, 5, 7, 6, 3):
                mats[i].start()
            for k in range(1, PARTS):
                h_load(k).start()

        px[c, :, 0:16] = jnp.zeros((3, 16, L), BF16)
        last = [px[c, i, TOK : TOK + 16].astype(F32)[14:16] for i in range(3)]
        tip[c] = jnp.concatenate(last + [jnp.zeros((10, L), F32)], axis=0).astype(BF16)

        @pl.when(has_next)
        def _():
            p_halo(c).start()

        @pl.loop(0, LT)
        def _(l):
            stream_rows(c, l)

        @pl.when(jnp.logical_and(has_next, c == 0))
        def _():
            gated_halo(c).start()

    @pl.when(has_next)
    def _():
        gated_halo(1).start()

    cot_start(1)
    mats[4].wait()

    def filter_transform(c):
        h_load(c).wait()
        h = hv[c]
        high = h.astype(BF16)
        hb[0:TAPS] = high
        hb[TAPS : 2 * TAPS] = high
        hb[2 * TAPS :] = (h - high.astype(F32)).astype(BF16)
        hslot = lax.rem(c, 3)
        hhat[hslot] = dot(f4[...], hb[...])
        hhat[hslot, 0:HALF] = hhat[hslot, 0:HALF] + skip_ref[0:1, lanes(c)]

    filter_transform(0)

    @pl.loop(0, PARTS)
    def _(c):
        @pl.when(has_previous)
        def _():
            p_halo(c).wait_recv()

        @pl.when(me == 0)
        def _():
            p_halo_ref[c] = jnp.zeros((16, L), BF16)

        before = p_halo_ref[c].astype(F32)
        out = []
        for i, keep in enumerate((qs, ks, vs)):
            x = jnp.concatenate([before[2 * i : 2 * i + 2], px[c, i, 16:32].astype(F32)], axis=0)
            s = sf_ref[i, 0:1, lanes(c)] * x[2:18]
            s = s + sf_ref[i, 1:2, lanes(c)] * x[1:17]
            s = s + sf_ref[i, 2:3, lanes(c)] * x[0:16]
            keep[c, 0:16] = s
            out.append(s)
        gated[c, 0:16] = (out[1] * out[2]).astype(BF16)

    def products(a, b, conj):
        @pl.loop(0, HALF // 16, unroll=2)
        def _(r):
            rows = pl.ds(pl.multiple_of(r * 16, 16), 16)
            rows_i = pl.ds(pl.multiple_of(HALF + r * 16, 16), 16)
            ar, ai, br, bi = a[rows], a[rows_i], b[rows], b[rows_i]
            if conj:
                re, im = ar * br + ai * bi, ai * br - ar * bi
            else:
                re, im = ar * br - ai * bi, ar * bi + ai * br
            for value, start in ((re, 0), (im, HALF)):
                high = value.astype(BF16)
                at = pl.multiple_of(start + r * 16, 16)
                yb[pl.ds(at, 16)] = high
                yb[pl.ds(POINTS + at, 16)] = (value - high.astype(F32)).astype(BF16)

    def back(matrix):
        return dot(matrix[:, : 2 * POINTS], yb[...]) + dot(matrix[:, 2 * POINTS :], yb[0:POINTS])

    def filter_and_mix(c):
        slot, hslot = lax.rem(c, 2), lax.rem(c, 3)
        own = gated[c]
        ghat[slot] = dot(f0[:, TAPS:], own) + dot(f1[:, TAPS:], own)

        @pl.when(has_previous)
        def _():
            gated_halo(c).wait_recv()

        @pl.when(me == 0)
        def _():
            g_halo[c] = jnp.zeros((TAPS, L), BF16)

        twice[0:TAPS] = g_halo[c]
        twice[TAPS:] = g_halo[c]
        ghat[slot] = ghat[slot] + dot(f2[...], twice[...])
        products(ghat.at[slot], hhat.at[hslot], False)
        mixed[slot] = back(f5)

    def multiply_cotangent(c):
        slot = lax.rem(c, 2)
        cot_own(c).wait()
        for k in (2, 1, 3):
            cot_wait(c, k)

        @pl.loop(0, TOK // 16, unroll=2)
        def _(r):
            rows = pl.ds(pl.multiple_of(r * 16, 16), 16)
            up = cot[c, rows].astype(F32)
            dm[c, rows] = (up * qs[c, rows]).astype(BF16)
            ds[c, 0, rows] = (up * mixed[slot, rows]).astype(BF16)

        @pl.when(has_previous)
        def _():
            mixed_halo(c).start()

    def filter_gradient(c):
        slot = lax.rem(c, 2)
        own = dm[c]
        dhat[slot] = dot(f0[:, :TOK], own) + dot(f1[:, :TOK], own)
        products(ghat.at[slot], dhat.at[slot], True)
        parts[c] = back(f7)

        @pl.loop(1, GROUP)
        def _(k):
            peer = lax.rem(g + k, GROUP)
            pltpu.make_async_remote_copy(
                src_ref=parts.at[c, pl.ds(pl.multiple_of(peer * 8, 8), 8)], dst_ref=landed.at[c, k - 1],
                send_sem=rs_sem.at[0, c], recv_sem=rs_sem.at[1, c], **to_seq(plane + peer)).start()

    def gated_gradient(c):
        slot, hslot = lax.rem(c, 2), lax.rem(c, 3)
        @pl.when(has_next)
        def _():
            mixed_halo(c).wait_recv()

        @pl.when(me == PEERS - 1)
        def _():
            dm_halo[c] = jnp.zeros((TAPS, L), BF16)

        twice[0:TAPS] = dm_halo[c]
        twice[TAPS:] = dm_halo[c]
        dhat[slot] = dhat[slot] + dot(f3[...], twice[...])
        products(dhat.at[slot], hhat.at[hslot], True)
        grad = back(f6)
        ds[c, 1, 0:TOK] = (grad * vs[c]).astype(BF16)
        ds[c, 2, 0:TOK] = (grad * ks[c]).astype(BF16)
        d_store(0, c).start()

        @pl.when(has_previous)
        def _():
            grad_halo(c).start()

    mine = pl.ds(pl.multiple_of(g * 8, 8), 8)

    def cross(c):
        return pltpu.make_async_remote_copy(
            src_ref=xs.at[c], dst_ref=xr.at[c], send_sem=xx_sem.at[0, c], recv_sem=xx_sem.at[1, c], **to_seq(across))

    def sum_plane(c):
        pltpu.make_async_copy(landed.at[c], landed.at[c], rs_sem.at[1, c]).wait()
        total = parts[c, mine]
        for k in range(GROUP - 1):
            total = total + landed[c, k]
        xs[c] = total
        cross(c).start()

    def spread(c):
        cross(c).wait_recv()
        total = (xs[c] + xr[c]) * (1.0 / 128.0)
        shared[c, g] = jnp.concatenate([total[:, : L // 2], total[:, L // 2 :]], axis=0).astype(BF16)

        @pl.loop(1, GROUP)
        def _(k):
            pltpu.make_async_remote_copy(
                src_ref=shared.at[c, g], dst_ref=shared.at[c, g],
                send_sem=ag_sem.at[0, c], recv_sem=ag_sem.at[1, c], **to_seq(mate(k))).start()

    def short_gradient(c):
        @pl.when(has_next)
        def _():
            grad_halo(c).wait_recv()

        @pl.when(me == PEERS - 1)
        def _():
            d_halo[c] = jnp.zeros((3, 16, L), BF16)

        halo_store(c).start()
        ds[c, :, TOK : TOK + 16] = d_halo[c]

        @pl.loop(0, 3 * LT)
        def _(n):
            i, l = n // LT, lax.rem(n, LT)
            cols = pl.ds(pl.multiple_of(l * 128, 128), 128)
            line[i] = ds[c, i, :, cols].astype(F32)

            def rows(b, acc):
                p = px[c, i, pl.ds(pl.multiple_of(16 + b * 64, 16), 64), cols].astype(F32)
                return tuple(
                    acc[j] + jnp.sum((line[i, pl.ds(b * 64 + j, 64)] * p).reshape(8, 8, 128), axis=0)
                    for j in range(SHORT))

            acc = lax.fori_loop(0, TOK // 64, rows, tuple(jnp.zeros((8, 128), F32) for _ in range(SHORT)), unroll=8)
            for j in range(SHORT):
                gs[c * LT + l, pl.ds(3 * i + j, 1)] = jnp.sum(acc[j], axis=0, keepdims=True)

        @pl.loop(0, 2 * LT)
        def _(n):
            owner = c * LT + lax.rem(n, LT)
            peer = owner + GROUP * (n // LT)

            @pl.when(peer != me)
            def _():
                pltpu.make_async_remote_copy(
                    src_ref=gs.at[owner], dst_ref=gs_landed.at[me],
                    send_sem=tail_sem.at[0], recv_sem=tail_sem.at[1], **to_seq(peer)).start()

    gs[...] = jnp.zeros(gs.shape, F32)
    for i in (0, 1, 2, 5):
        mats[i].wait()
    filter_and_mix(0)
    for i in (7, 6, 3):
        mats[i].wait()

    @pl.loop(0, PARTS + 2)
    def _(s):
        @pl.when(s < PARTS)
        def _():
            multiply_cotangent(s)

        @pl.when(s < PARTS)
        def _():
            filter_gradient(s)

        @pl.when(s + 2 < PARTS)
        def _():
            @pl.when(has_next)
            def _():
                gated_halo(s + 2).start()

            cot_start(s + 2)

        @pl.when(s + 1 < PARTS)
        def _():
            filter_transform(s + 1)
            filter_and_mix(s + 1)

        @pl.when(jnp.logical_and(s >= 2, s <= PARTS))
        def _():
            sum_plane(s - 2)

        @pl.when(jnp.logical_and(s >= 1, s <= PARTS))
        def _():
            gated_gradient(s - 1)

        @pl.when(jnp.logical_and(s >= 2, s <= PARTS))
        def _():
            spread(s - 2)

        @pl.when(s == PARTS)
        def _():
            sum_plane(PARTS - 1)

        @pl.when(s == PARTS + 1)
        def _():
            spread(PARTS - 1)

        @pl.when(s >= 2)
        def _():
            short_gradient(s - 2)

    def finish_stream(i):
        @pl.loop(0, PARTS * LT)
        def _(n):
            c, l = n // LT, lax.rem(n, LT)
            cols = pl.ds(pl.multiple_of(l * 128, 128), 128)
            wide = pl.ds(pl.multiple_of(n * 128, 128), 128)
            line[i] = ds[c, i, :, cols].astype(F32)
            taps = [sf_ref[i, j : j + 1, wide] for j in range(SHORT)]

            @pl.loop(0, TOK // 64, unroll=4)
            def _(r):
                result = taps[0] * line[i, pl.ds(r * 64, 64)]
                for j in range(1, SHORT):
                    result = result + taps[j] * line[i, pl.ds(r * 64 + j, 64)]
                ds[c, i, pl.ds(pl.multiple_of(r * 64, 64), 64), cols] = result.astype(BF16)

            @pl.when(l == LT - 1)
            def _():
                d_store(i, c).start()

    @pl.when(has_previous)
    def _():
        for c in range(PARTS):
            grad_halo(c).wait_send()

    finish_stream(2)
    gs_landed[me] = gs[g]
    others = gs_landed.at[0 : PEERS - 1]
    mates = gs_landed.at[0 : GROUP - 1]
    pltpu.make_async_copy(others, others, tail_sem.at[1]).wait()
    total = gs_landed[0]
    for k in range(1, PEERS):
        total = total + gs_landed[k]
    gs_sums[g] = total * (1.0 / 128.0)

    @pl.loop(1, GROUP)
    def _(k):
        pltpu.make_async_remote_copy(
            src_ref=gs_sums.at[g], dst_ref=gs_sums.at[g],
            send_sem=tail_sem.at[2], recv_sem=tail_sem.at[3], **to_seq(mate(k))).start()

    finish_stream(1)

    def gl_store(c):
        return pltpu.make_async_copy(sums.at[c], gl_out.at[:, lanes(c)], h_sem.at[c])

    @pl.loop(0, PARTS)
    def _(c):
        fifteen = shared.at[c, 0 : GROUP - 1]
        pltpu.make_async_copy(fifteen, fifteen, ag_sem.at[1, c]).wait()
        for p in range(GROUP):
            piece = shared[c, p].astype(F32)
            sums[c, 8 * p : 8 * p + 8, : L // 2] = piece[0:8]
            sums[c, 8 * p : 8 * p + 8, L // 2 :] = piece[8:16]
        gl_store(c).start()
        for k in (2, 1, 3):
            cot_send(c, k).wait_send()

        @pl.when(has_next)
        def _():
            p_halo(c).wait_send()
            gated_halo(c).wait_send()

        @pl.when(has_previous)
        def _():
            mixed_halo(c).wait_send()

        cross(c).wait_send()
        pltpu.make_async_copy(landed.at[c], landed.at[c], rs_sem.at[0, c]).wait()
        pltpu.make_async_copy(fifteen, fifteen, ag_sem.at[0, c]).wait()
        for i in range(3):
            d_store(i, c).wait()
        halo_store(c).wait()
        gl_store(c).wait()

    pltpu.make_async_copy(others, others, tail_sem.at[0]).wait()
    pltpu.make_async_copy(mates, mates, tail_sem.at[3]).wait()
    pltpu.make_async_copy(mates, mates, tail_sem.at[2]).wait()
    gs_out[...] = gs_sums[...]


ROWS = 256


def finish_kernel(sf_ref, d_ref, more_ref, gl_ref, gs_ref, gi_out, gl_out, skip_out, gs_out, line):
    i, b = pl.program_id(0), pl.program_id(1)

    @pl.when(i < 1)
    def _():
        @pl.loop(0, CH // 512)
        def _(quarter):
            for k in range(4):
                cols = pl.ds(pl.multiple_of(quarter * 512 + k * 128, 128), 128)
                line[k, 0:ROWS] = d_ref[0, :, cols].astype(F32)
                line[k, ROWS:] = more_ref[0, :, cols].astype(F32)
            for k in range(4):
                cols = pl.ds(pl.multiple_of(quarter * 512 + k * 128, 128), 128)
                taps = [sf_ref[i, j : j + 1, cols] for j in range(SHORT)]

                @pl.loop(0, ROWS // 64, unroll=4)
                def _(r):
                    result = taps[0] * line[k, pl.ds(r * 64, 64)]
                    for j in range(1, SHORT):
                        result = result + taps[j] * line[k, pl.ds(r * 64 + j, 64)]
                    gi_out[0, pl.ds(pl.multiple_of(r * 64, 64), 64), cols] = result.astype(BF16)

    @pl.when(i >= 1)
    def _():
        gi_out[...] = d_ref[...]

    @pl.when(i == 0)
    def _():
        gl_out[...] = gl_ref[...]

    @pl.when(jnp.logical_and(i == 0, b == 0))
    def _():
        skip_out[...] = gl_ref[0]
        for stream in range(3):
            for j in range(SHORT):
                row = 3 * stream + j
                gs_out[stream, j : j + 1] = jnp.concatenate(
                    [gs_ref[t, row : row + 1] for t in range(GROUP)], axis=1)


def finish(short_filters, d, gl, gs):
    whole = lambda shape: pl.BlockSpec(shape, lambda i, b: (0,) * len(shape))
    steps = TOK // ROWS
    turn = pl.BlockSpec((TAPS // steps, CH), lambda i, b: (jnp.where(i == 0, b, steps - 1), 0))
    return pl.pallas_call(
        finish_kernel,
        grid=(3, steps),
        out_shape=(
            jax.ShapeDtypeStruct((3, TOK, CH), BF16),
            jax.ShapeDtypeStruct((TAPS, CH), F32),
            jax.ShapeDtypeStruct((CH,), F32),
            jax.ShapeDtypeStruct((3, SHORT, CH), F32),
        ),
        in_specs=[
            whole((3, SHORT, CH)),
            pl.BlockSpec((1, ROWS, CH), lambda i, b: (i, b, 0)),
            pl.BlockSpec((1, 16, CH), lambda i, b: (i, (b + 1) * (ROWS // 16), 0)),
            turn,
            whole((GROUP, 16, 128)),
        ],
        out_specs=(
            pl.BlockSpec((1, ROWS, CH), lambda i, b: (i, b, 0)),
            turn,
            whole((CH,)),
            whole((3, SHORT, CH)),
        ),
        scratch_shapes=[pltpu.VMEM((4, ROWS + 16, 128), F32)],
        compiler_params=pltpu.CompilerParams(vmem_limit_bytes=60 << 20),
        cost_estimate=pl.CostEstimate(flops=2 * 10**7, bytes_accessed=16 * 10**6, transcendentals=0),
    )(short_filters, d, d, gl, gs)


def per_device(projected, short_filters, long_filter, skip_gain, cotangent):
    mats = [jnp.asarray(m) for m in matrices()]
    anywhere = pl.BlockSpec(memory_space=pl.ANY)
    vmem = pl.BlockSpec(memory_space=pltpu.VMEM)
    dma = pltpu.SemaphoreType.DMA
    scratch = [
        pltpu.VMEM((PARTS, 3, TOK + 16, L), BF16),
        pltpu.VMEM((PARTS, 16, L), BF16),
        pltpu.VMEM((PARTS, 16, L), BF16),
        pltpu.VMEM((PARTS, TOK, L), F32),
        pltpu.VMEM((PARTS, TOK, L), F32),
        pltpu.VMEM((PARTS, TOK, L), F32),
        pltpu.VMEM((PARTS, TOK, L), BF16),
        pltpu.VMEM((PARTS, TAPS, L), BF16),
        pltpu.VMEM((2, POINTS, L), F32),
        pltpu.VMEM((3, POINTS, L), F32),
        pltpu.VMEM((2, TOK, L), F32),
        pltpu.VMEM((PARTS, TOK, L), BF16),
        pltpu.VMEM((PARTS, TOK, L), BF16),
        pltpu.VMEM((PARTS, TAPS, L), BF16),
        pltpu.VMEM((2, POINTS, L), F32),
        pltpu.VMEM((PARTS, 3, TOK + 16, L), BF16),
        pltpu.VMEM((PARTS, 3, 16, L), BF16),
        pltpu.VMEM((2 * POINTS, L), BF16),
        pltpu.VMEM((3 * TAPS, L), BF16),
        pltpu.VMEM((2 * TAPS, L), BF16),
        pltpu.VMEM((3, TOK + 16, 128), F32),
        pltpu.VMEM((PARTS, TAPS, L), F32),
        *[pltpu.VMEM(m.shape, BF16) for m in mats],
        pltpu.VMEM((PARTS, TAPS, L), F32),
        pltpu.VMEM((PARTS, GROUP - 1, 8, L), F32),
        pltpu.VMEM((PARTS, 8, L), F32),
        pltpu.VMEM((PARTS, 8, L), F32),
        pltpu.VMEM((PARTS, GROUP, 16, L // 2), BF16),
        pltpu.VMEM((PARTS, TAPS, L), F32),
        pltpu.VMEM((GROUP, 16, 128), F32),
        pltpu.VMEM((PEERS, 16, 128), F32),
        pltpu.VMEM((GROUP, 16, 128), F32),
        dma((PARTS,)),
        dma((len(mats),)),
        dma((PARTS,)),
        dma((PARTS,)),
        dma((3, PARTS)),
        dma((PARTS,)),
        dma((PARTS, 3)),
        dma((PARTS, 3)),
        *[dma((2, PARTS)) for _ in range(7)],
        dma((4,)),
    ]
    d, gl, gs = pl.pallas_call(
        kernel,
        out_shape=(
            jax.ShapeDtypeStruct((3, TOK + 16, CH), BF16),
            jax.ShapeDtypeStruct((TAPS, CH), F32),
            jax.ShapeDtypeStruct((GROUP, 16, 128), F32),
        ),
        in_specs=[anywhere, vmem, anywhere, vmem, anywhere] + [anywhere] * len(mats),
        out_specs=(anywhere, anywhere, vmem),
        scratch_shapes=scratch,
        compiler_params=pltpu.CompilerParams(collective_id=0, has_side_effects=True, vmem_limit_bytes=62 << 20),
        cost_estimate=pl.CostEstimate(flops=20 * 10**9, bytes_accessed=24 * 10**6, transcendentals=0),
    )(projected, short_filters, long_filter, skip_gain[None], cotangent, *mats)
    return finish(short_filters, d, gl, gs)


def solution(mesh):
    placed = (
        P(None, "seq", "ch"),
        P(None, None, "ch"),
        P(None, "ch"),
        P("ch"),
        P(("seq", "ch"), None),
    )
    return jax.shard_map(
        per_device,
        mesh=mesh,
        in_specs=placed,
        out_specs=(P(None, "seq", "ch"), P(None, "ch"), P("ch"), P(None, None, "ch")),
        check_vma=False,
    )
```

```python
import functools

import jax
import jax.numpy as jnp
import numpy as np
from jax import lax
from jax.experimental import pallas as pl
from jax.experimental.pallas import tpu as pltpu
from jax.sharding import PartitionSpec as P

TAPS = 128
SHORT = 3
TOK = 512
CH = 2048
POINTS = TOK + TAPS
HALF = POINTS // 2
GROUP = 16
PEERS = 32
PARTS = 4
L = CH // PARTS
LT = L // 128
MESH = pl.DeviceIdType.MESH
F32, BF16 = jnp.float32, jnp.bfloat16


def split(x):
    high = x.astype(np.float32).astype(BF16)
    return high, (x - high.astype(np.float64)).astype(np.float32).astype(BF16)


@functools.cache
def matrices():
    angle = 2 * np.pi * np.outer(np.arange(HALF) + 0.5, np.arange(POINTS)) / POINTS
    forward = np.concatenate([np.cos(angle), -np.sin(angle)])
    inverse = (2.0 / POINTS) * np.concatenate([np.cos(angle.T), -np.sin(angle.T)], axis=1)
    fh, fl = split(forward)
    cat = lambda *parts: np.concatenate(parts, axis=1)
    first, last = slice(0, TAPS), slice(TOK, POINTS)

    def back(rows):
        high, low = split(inverse[rows])
        return cat(high, high, low)

    return (
        fh,
        fl,
        cat(fh[:, first], fl[:, first]),
        cat(fh[:, last], fl[:, last]),
        cat(fh[:, first], fl[:, first], fh[:, first]),
        back(np.arange(TAPS, POINTS)),
        back(np.arange(TOK)),
        back(TAPS - np.arange(TAPS)),
    )


def dot(a, b):
    return jnp.dot(a, b, preferred_element_type=F32)


def kernel(
    proj, sf_ref, h_hbm, skip_ref, cot_hbm, m0, m1, m2, m3, m4, m5, m6, m7,
    d_out, gl_out, gs_out,
    px, tip, p_halo_ref, qs, ks, vs, gated, g_halo, ghat, hhat, mixed, cot, dm, dm_halo, dhat, ds, d_halo,
    yb, hb, twice, line, hv, f0, f1, f2, f3, f4, f5, f6, f7,
    parts, landed, xs, xr, shared, sums, gs, gs_landed, gs_sums,
    load_sem, mat_sem, h_sem, own_sem, out_sem, halo_out_sem, a2a_send, a2a_recv,
    ph_sem, gh_sem, dmh_sem, dh_sem, rs_sem, xx_sem, ag_sem, tail_sem,
):
    me = lax.axis_index("seq")
    col = lax.axis_index("ch")
    g = lax.rem(me, GROUP)
    plane = me - g
    nxt, prv = lax.rem(me + 1, PEERS), lax.rem(me + PEERS - 1, PEERS)
    across = lax.rem(me + GROUP, PEERS)
    barrier = pltpu.get_barrier_semaphore()

    def to_seq(s):
        return dict(device_id={"seq": s}, device_id_type=MESH)

    def to_ch(c):
        return dict(device_id={"ch": c}, device_id_type=MESH)

    def mate(k):
        return plane + lax.rem(g + k, GROUP)

    def lanes(c):
        return pl.ds(pl.multiple_of(c * L, L), L)

    def p_load(c):
        return pltpu.make_async_copy(proj.at[:, :, lanes(c)], px.at[c, :, 16 : 16 + TOK], load_sem.at[c])

    def h_load(c):
        return pltpu.make_async_copy(h_hbm.at[:, lanes(c)], hv.at[c], h_sem.at[c])

    mats = [
        pltpu.make_async_copy(a, b, mat_sem.at[i])
        for i, (a, b) in enumerate(zip((m0, m1, m2, m3, m4, m5, m6, m7), (f0, f1, f2, f3, f4, f5, f6, f7)))
    ]
    p_load(0).start()
    p_load(1).start()

    @pl.loop(1, PEERS)
    def _(k):
        pl.semaphore_signal(barrier, inc=1, **to_seq(lax.rem(me + k, PEERS)))

    for k in range(1, 4):
        pl.semaphore_signal(barrier, inc=1, **to_ch(lax.rem(col + k, 4)))


    def cot_block(c, owner):
        return cot.at[c, pl.ds(pl.multiple_of(owner * 128, 128), 128)]

    def cot_own(c):
        cols = pl.ds(pl.multiple_of(col * CH + c * L, L), L)
        return pltpu.make_async_copy(cot_hbm.at[:, cols], cot_block(c, col), own_sem.at[c])

    def cot_send(c, k):
        peer = lax.rem(col + k, 4)
        cols = pl.ds(pl.multiple_of(peer * CH + c * L, L), L)
        return pltpu.make_async_remote_copy(
            src_ref=cot_hbm.at[:, cols], dst_ref=cot_block(c, col),
            send_sem=a2a_send.at[c, k - 1], recv_sem=a2a_recv.at[c, k - 1], **to_ch(peer))

    def cot_wait(c, k):
        block = cot_block(c, lax.rem(col + 4 - k, 4))
        pltpu.make_async_copy(block, block, a2a_recv.at[c, k - 1]).wait()

    def p_halo(c):
        return pltpu.make_async_remote_copy(
            src_ref=tip.at[c], dst_ref=p_halo_ref.at[c],
            send_sem=ph_sem.at[0, c], recv_sem=ph_sem.at[1, c], **to_seq(nxt))

    def gated_halo(c):
        return pltpu.make_async_remote_copy(
            src_ref=gated.at[c, TOK - TAPS : TOK], dst_ref=g_halo.at[c],
            send_sem=gh_sem.at[0, c], recv_sem=gh_sem.at[1, c], **to_seq(nxt))

    def mixed_halo(c):
        return pltpu.make_async_remote_copy(
            src_ref=dm.at[c, 0:TAPS], dst_ref=dm_halo.at[c],
            send_sem=dmh_sem.at[0, c], recv_sem=dmh_sem.at[1, c], **to_seq(prv))

    def grad_halo(c):
        return pltpu.make_async_remote_copy(
            src_ref=ds.at[c, :, 0:16], dst_ref=d_halo.at[c],
            send_sem=dh_sem.at[0, c], recv_sem=dh_sem.at[1, c], **to_seq(prv))

    def d_store(i, c):
        return pltpu.make_async_copy(ds.at[c, i, 0:TOK], d_out.at[i, 0:TOK, lanes(c)], out_sem.at[i, c])

    def halo_store(c):
        return pltpu.make_async_copy(d_halo.at[c], d_out.at[:, TOK : TOK + 16, lanes(c)], halo_out_sem.at[c])

    def cot_start(c):
        cot_own(c).start()
        for k in (2, 1, 3):
            cot_send(c, k).start()

    has_next, has_previous = me < PEERS - 1, me > 0

    def stream_rows(c, l):
        cols = pl.ds(pl.multiple_of(l * 128, 128), 128)
        wide = pl.ds(pl.multiple_of(c * L + l * 128, 128), 128)
        for i in range(3):
            line[i] = px[c, i, :, cols].astype(F32)
        taps = [[sf_ref[i, j : j + 1, wide] for j in range(SHORT)] for i in range(3)]

        @pl.loop(0, TOK // 64, unroll=4)
        def _(b):
            here = pl.ds(pl.multiple_of(b * 64, 64), 64)
            out = []
            for i, keep in enumerate((qs, ks, vs)):
                s = taps[i][0] * line[i, pl.ds(b * 64 + 16, 64)]
                s = s + taps[i][1] * line[i, pl.ds(b * 64 + 15, 64)]
                s = s + taps[i][2] * line[i, pl.ds(b * 64 + 14, 64)]
                keep[c, here, cols] = s
                out.append(s)
            gated[c, here, cols] = (out[1] * out[2]).astype(BF16)

    pl.semaphore_wait(barrier, PEERS - 1 + 3)
    cot_start(0)

    @pl.loop(0, PARTS)
    def _(c):
        p_load(c).wait()

        @pl.when(c + 2 < PARTS)
        def _():
            p_load(c + 2).start()

        @pl.when(c == 0)
        def _():
            h_load(0).start()
            mats[4].start()

        @pl.when(c == 1)
        def _():
            for i in (0, 1, 2, 5, 7, 6, 3):
                mats[i].start()
            for k in range(1, PARTS):
                h_load(k).start()

        px[c, :, 0:16] = jnp.zeros((3, 16, L), BF16)
        last = [px[c, i, TOK : TOK + 16].astype(F32)[14:16] for i in range(3)]
        tip[c] = jnp.concatenate(last + [jnp.zeros((10, L), F32)], axis=0).astype(BF16)

        @pl.when(has_next)
        def _():
            p_halo(c).start()

        @pl.loop(0, LT)
        def _(l):
            stream_rows(c, l)

        @pl.when(jnp.logical_and(has_next, c == 0))
        def _():
            gated_halo(c).start()

    @pl.when(has_next)
    def _():
        gated_halo(1).start()

    cot_start(1)
    mats[4].wait()

    def filter_transform(c):
        h_load(c).wait()
        h = hv[c]
        high = h.astype(BF16)
        hb[0:TAPS] = high
        hb[TAPS : 2 * TAPS] = high
        hb[2 * TAPS :] = (h - high.astype(F32)).astype(BF16)
        hslot = lax.rem(c, 3)
        hhat[hslot] = dot(f4[...], hb[...])
        hhat[hslot, 0:HALF] = hhat[hslot, 0:HALF] + skip_ref[0:1, lanes(c)]

    filter_transform(0)

    @pl.loop(0, PARTS)
    def _(c):
        @pl.when(has_previous)
        def _():
            p_halo(c).wait_recv()

        @pl.when(me == 0)
        def _():
            p_halo_ref[c] = jnp.zeros((16, L), BF16)

        before = p_halo_ref[c].astype(F32)
        out = []
        for i, keep in enumerate((qs, ks, vs)):
            x = jnp.concatenate([before[2 * i : 2 * i + 2], px[c, i, 16:32].astype(F32)], axis=0)
            s = sf_ref[i, 0:1, lanes(c)] * x[2:18]
            s = s + sf_ref[i, 1:2, lanes(c)] * x[1:17]
            s = s + sf_ref[i, 2:3, lanes(c)] * x[0:16]
            keep[c, 0:16] = s
            out.append(s)
        gated[c, 0:16] = (out[1] * out[2]).astype(BF16)

    def products(a, b, conj):
        @pl.loop(0, HALF // 16, unroll=2)
        def _(r):
            rows = pl.ds(pl.multiple_of(r * 16, 16), 16)
            rows_i = pl.ds(pl.multiple_of(HALF + r * 16, 16), 16)
            ar, ai, br, bi = a[rows], a[rows_i], b[rows], b[rows_i]
            if conj:
                re, im = ar * br + ai * bi, ai * br - ar * bi
            else:
                re, im = ar * br - ai * bi, ar * bi + ai * br
            for value, start in ((re, 0), (im, HALF)):
                high = value.astype(BF16)
                at = pl.multiple_of(start + r * 16, 16)
                yb[pl.ds(at, 16)] = high
                yb[pl.ds(POINTS + at, 16)] = (value - high.astype(F32)).astype(BF16)

    def back(matrix):
        return dot(matrix[:, : 2 * POINTS], yb[...]) + dot(matrix[:, 2 * POINTS :], yb[0:POINTS])

    def filter_and_mix(c):
        slot, hslot = lax.rem(c, 2), lax.rem(c, 3)
        own = gated[c]
        ghat[slot] = dot(f0[:, TAPS:], own) + dot(f1[:, TAPS:], own)

        @pl.when(has_previous)
        def _():
            gated_halo(c).wait_recv()

        @pl.when(me == 0)
        def _():
            g_halo[c] = jnp.zeros((TAPS, L), BF16)

        twice[0:TAPS] = g_halo[c]
        twice[TAPS:] = g_halo[c]
        ghat[slot] = ghat[slot] + dot(f2[...], twice[...])
        products(ghat.at[slot], hhat.at[hslot], False)
        mixed[slot] = back(f5)

    def multiply_cotangent(c):
        slot = lax.rem(c, 2)
        cot_own(c).wait()
        for k in (2, 1, 3):
            cot_wait(c, k)

        @pl.loop(0, TOK // 16, unroll=2)
        def _(r):
            rows = pl.ds(pl.multiple_of(r * 16, 16), 16)
            up = cot[c, rows].astype(F32)
            dm[c, rows] = (up * qs[c, rows]).astype(BF16)
            ds[c, 0, rows] = (up * mixed[slot, rows]).astype(BF16)

        @pl.when(has_previous)
        def _():
            mixed_halo(c).start()

    def filter_gradient(c):
        slot = lax.rem(c, 2)
        own = dm[c]
        dhat[slot] = dot(f0[:, :TOK], own) + dot(f1[:, :TOK], own)
        products(ghat.at[slot], dhat.at[slot], True)
        parts[c] = back(f7)

        @pl.loop(1, GROUP)
        def _(k):
            peer = lax.rem(g + k, GROUP)
            pltpu.make_async_remote_copy(
                src_ref=parts.at[c, pl.ds(pl.multiple_of(peer * 8, 8), 8)], dst_ref=landed.at[c, k - 1],
                send_sem=rs_sem.at[0, c], recv_sem=rs_sem.at[1, c], **to_seq(plane + peer)).start()

    def gated_gradient(c):
        slot, hslot = lax.rem(c, 2), lax.rem(c, 3)
        @pl.when(has_next)
        def _():
            mixed_halo(c).wait_recv()

        @pl.when(me == PEERS - 1)
        def _():
            dm_halo[c] = jnp.zeros((TAPS, L), BF16)

        twice[0:TAPS] = dm_halo[c]
        twice[TAPS:] = dm_halo[c]
        dhat[slot] = dhat[slot] + dot(f3[...], twice[...])
        products(dhat.at[slot], hhat.at[hslot], True)
        grad = back(f6)
        ds[c, 1, 0:TOK] = (grad * vs[c]).astype(BF16)
        ds[c, 2, 0:TOK] = (grad * ks[c]).astype(BF16)
        d_store(0, c).start()

        @pl.when(has_previous)
        def _():
            grad_halo(c).start()

    mine = pl.ds(pl.multiple_of(g * 8, 8), 8)

    def cross(c):
        return pltpu.make_async_remote_copy(
            src_ref=xs.at[c], dst_ref=xr.at[c], send_sem=xx_sem.at[0, c], recv_sem=xx_sem.at[1, c], **to_seq(across))

    def sum_plane(c):
        pltpu.make_async_copy(landed.at[c], landed.at[c], rs_sem.at[1, c]).wait()
        total = parts[c, mine]
        for k in range(GROUP - 1):
            total = total + landed[c, k]
        xs[c] = total
        cross(c).start()

    def spread(c):
        cross(c).wait_recv()
        total = (xs[c] + xr[c]) * (1.0 / 128.0)
        shared[c, g] = jnp.concatenate([total[:, : L // 2], total[:, L // 2 :]], axis=0).astype(BF16)

        @pl.loop(1, GROUP)
        def _(k):
            pltpu.make_async_remote_copy(
                src_ref=shared.at[c, g], dst_ref=shared.at[c, g],
                send_sem=ag_sem.at[0, c], recv_sem=ag_sem.at[1, c], **to_seq(mate(k))).start()

    def short_gradient(c):
        @pl.when(has_next)
        def _():
            grad_halo(c).wait_recv()

        @pl.when(me == PEERS - 1)
        def _():
            d_halo[c] = jnp.zeros((3, 16, L), BF16)

        halo_store(c).start()
        ds[c, :, TOK : TOK + 16] = d_halo[c]

        @pl.loop(0, 3 * LT)
        def _(n):
            i, l = n // LT, lax.rem(n, LT)
            cols = pl.ds(pl.multiple_of(l * 128, 128), 128)
            line[i] = ds[c, i, :, cols].astype(F32)

            def rows(b, acc):
                p = px[c, i, pl.ds(pl.multiple_of(16 + b * 64, 16), 64), cols].astype(F32)
                return tuple(
                    acc[j] + jnp.sum((line[i, pl.ds(b * 64 + j, 64)] * p).reshape(8, 8, 128), axis=0)
                    for j in range(SHORT))

            acc = lax.fori_loop(0, TOK // 64, rows, tuple(jnp.zeros((8, 128), F32) for _ in range(SHORT)), unroll=8)
            for j in range(SHORT):
                gs[c * LT + l, pl.ds(3 * i + j, 1)] = jnp.sum(acc[j], axis=0, keepdims=True)

        @pl.loop(0, 2 * LT)
        def _(n):
            owner = c * LT + lax.rem(n, LT)
            peer = owner + GROUP * (n // LT)

            @pl.when(peer != me)
            def _():
                pltpu.make_async_remote_copy(
                    src_ref=gs.at[owner], dst_ref=gs_landed.at[me],
                    send_sem=tail_sem.at[0], recv_sem=tail_sem.at[1], **to_seq(peer)).start()

    gs[...] = jnp.zeros(gs.shape, F32)
    for i in (0, 1, 2, 5):
        mats[i].wait()
    filter_and_mix(0)
    for i in (7, 6, 3):
        mats[i].wait()

    @pl.loop(0, PARTS + 2)
    def _(s):
        @pl.when(s < PARTS)
        def _():
            multiply_cotangent(s)

        @pl.when(s < PARTS)
        def _():
            filter_gradient(s)

        @pl.when(s + 2 < PARTS)
        def _():
            @pl.when(has_next)
            def _():
                gated_halo(s + 2).start()

        @pl.when(s + 1 < PARTS)
        def _():
            filter_transform(s + 1)
            filter_and_mix(s + 1)

        @pl.when(s + 2 < PARTS)
        def _():
            cot_start(s + 2)

        @pl.when(jnp.logical_and(s >= 2, s <= PARTS))
        def _():
            sum_plane(s - 2)

        @pl.when(jnp.logical_and(s >= 1, s <= PARTS))
        def _():
            gated_gradient(s - 1)

        @pl.when(jnp.logical_and(s >= 2, s <= PARTS))
        def _():
            spread(s - 2)

        @pl.when(s == PARTS)
        def _():
            sum_plane(PARTS - 1)

        @pl.when(s == PARTS + 1)
        def _():
            spread(PARTS - 1)

        @pl.when(s >= 2)
        def _():
            short_gradient(s - 2)

    def finish_stream(i):
        @pl.loop(0, PARTS * LT)
        def _(n):
            c, l = n // LT, lax.rem(n, LT)
            cols = pl.ds(pl.multiple_of(l * 128, 128), 128)
            wide = pl.ds(pl.multiple_of(n * 128, 128), 128)
            line[i] = ds[c, i, :, cols].astype(F32)
            taps = [sf_ref[i, j : j + 1, wide] for j in range(SHORT)]

            @pl.loop(0, TOK // 64, unroll=4)
            def _(r):
                result = taps[0] * line[i, pl.ds(r * 64, 64)]
                for j in range(1, SHORT):
                    result = result + taps[j] * line[i, pl.ds(r * 64 + j, 64)]
                ds[c, i, pl.ds(pl.multiple_of(r * 64, 64), 64), cols] = result.astype(BF16)

            @pl.when(l == LT - 1)
            def _():
                d_store(i, c).start()

    @pl.when(has_previous)
    def _():
        for c in range(PARTS):
            grad_halo(c).wait_send()

    finish_stream(2)
    gs_landed[me] = gs[g]
    others = gs_landed.at[0 : PEERS - 1]
    mates = gs_landed.at[0 : GROUP - 1]
    pltpu.make_async_copy(others, others, tail_sem.at[1]).wait()
    total = gs_landed[0]
    for k in range(1, PEERS):
        total = total + gs_landed[k]
    gs_sums[g] = total * (1.0 / 128.0)

    @pl.loop(1, GROUP)
    def _(k):
        pltpu.make_async_remote_copy(
            src_ref=gs_sums.at[g], dst_ref=gs_sums.at[g],
            send_sem=tail_sem.at[2], recv_sem=tail_sem.at[3], **to_seq(mate(k))).start()

    finish_stream(1)

    def gl_store(c):
        return pltpu.make_async_copy(sums.at[c], gl_out.at[:, lanes(c)], h_sem.at[c])

    @pl.loop(0, PARTS)
    def _(c):
        fifteen = shared.at[c, 0 : GROUP - 1]
        pltpu.make_async_copy(fifteen, fifteen, ag_sem.at[1, c]).wait()
        for p in range(GROUP):
            piece = shared[c, p].astype(F32)
            sums[c, 8 * p : 8 * p + 8, : L // 2] = piece[0:8]
            sums[c, 8 * p : 8 * p + 8, L // 2 :] = piece[8:16]
        gl_store(c).start()
        for k in (2, 1, 3):
            cot_send(c, k).wait_send()

        @pl.when(has_next)
        def _():
            p_halo(c).wait_send()
            gated_halo(c).wait_send()

        @pl.when(has_previous)
        def _():
            mixed_halo(c).wait_send()

        cross(c).wait_send()
        pltpu.make_async_copy(landed.at[c], landed.at[c], rs_sem.at[0, c]).wait()
        pltpu.make_async_copy(fifteen, fifteen, ag_sem.at[0, c]).wait()
        for i in range(3):
            d_store(i, c).wait()
        halo_store(c).wait()
        gl_store(c).wait()

    pltpu.make_async_copy(others, others, tail_sem.at[0]).wait()
    pltpu.make_async_copy(mates, mates, tail_sem.at[3]).wait()
    pltpu.make_async_copy(mates, mates, tail_sem.at[2]).wait()
    gs_out[...] = gs_sums[...]


ROWS = 256


def finish_kernel(sf_ref, d_ref, more_ref, gl_ref, gs_ref, gi_out, gl_out, skip_out, gs_out, line):
    i, b = pl.program_id(0), pl.program_id(1)

    @pl.when(i < 1)
    def _():
        @pl.loop(0, CH // 512)
        def _(quarter):
            for k in range(4):
                cols = pl.ds(pl.multiple_of(quarter * 512 + k * 128, 128), 128)
                line[k, 0:ROWS] = d_ref[0, :, cols].astype(F32)
                line[k, ROWS:] = more_ref[0, :, cols].astype(F32)
            for k in range(4):
                cols = pl.ds(pl.multiple_of(quarter * 512 + k * 128, 128), 128)
                taps = [sf_ref[i, j : j + 1, cols] for j in range(SHORT)]

                @pl.loop(0, ROWS // 64, unroll=4)
                def _(r):
                    result = taps[0] * line[k, pl.ds(r * 64, 64)]
                    for j in range(1, SHORT):
                        result = result + taps[j] * line[k, pl.ds(r * 64 + j, 64)]
                    gi_out[0, pl.ds(pl.multiple_of(r * 64, 64), 64), cols] = result.astype(BF16)

    @pl.when(i >= 1)
    def _():
        gi_out[...] = d_ref[...]

    @pl.when(i == 0)
    def _():
        gl_out[...] = gl_ref[...]

    @pl.when(jnp.logical_and(i == 0, b == 0))
    def _():
        skip_out[...] = gl_ref[0]
        for stream in range(3):
            for j in range(SHORT):
                row = 3 * stream + j
                gs_out[stream, j : j + 1] = jnp.concatenate(
                    [gs_ref[t, row : row + 1] for t in range(GROUP)], axis=1)


def finish(short_filters, d, gl, gs):
    whole = lambda shape: pl.BlockSpec(shape, lambda i, b: (0,) * len(shape))
    steps = TOK // ROWS
    turn = pl.BlockSpec((TAPS // steps, CH), lambda i, b: (jnp.where(i == 0, b, steps - 1), 0))
    return pl.pallas_call(
        finish_kernel,
        grid=(3, steps),
        out_shape=(
            jax.ShapeDtypeStruct((3, TOK, CH), BF16),
            jax.ShapeDtypeStruct((TAPS, CH), F32),
            jax.ShapeDtypeStruct((CH,), F32),
            jax.ShapeDtypeStruct((3, SHORT, CH), F32),
        ),
        in_specs=[
            whole((3, SHORT, CH)),
            pl.BlockSpec((1, ROWS, CH), lambda i, b: (i, b, 0)),
            pl.BlockSpec((1, 16, CH), lambda i, b: (i, (b + 1) * (ROWS // 16), 0)),
            turn,
            whole((GROUP, 16, 128)),
        ],
        out_specs=(
            pl.BlockSpec((1, ROWS, CH), lambda i, b: (i, b, 0)),
            turn,
            whole((CH,)),
            whole((3, SHORT, CH)),
        ),
        scratch_shapes=[pltpu.VMEM((4, ROWS + 16, 128), F32)],
        compiler_params=pltpu.CompilerParams(vmem_limit_bytes=60 << 20),
        cost_estimate=pl.CostEstimate(flops=2 * 10**7, bytes_accessed=16 * 10**6, transcendentals=0),
    )(short_filters, d, d, gl, gs)


def per_device(projected, short_filters, long_filter, skip_gain, cotangent):
    mats = [jnp.asarray(m) for m in matrices()]
    anywhere = pl.BlockSpec(memory_space=pl.ANY)
    vmem = pl.BlockSpec(memory_space=pltpu.VMEM)
    dma = pltpu.SemaphoreType.DMA
    scratch = [
        pltpu.VMEM((PARTS, 3, TOK + 16, L), BF16),
        pltpu.VMEM((PARTS, 16, L), BF16),
        pltpu.VMEM((PARTS, 16, L), BF16),
        pltpu.VMEM((PARTS, TOK, L), F32),
        pltpu.VMEM((PARTS, TOK, L), F32),
        pltpu.VMEM((PARTS, TOK, L), F32),
        pltpu.VMEM((PARTS, TOK, L), BF16),
        pltpu.VMEM((PARTS, TAPS, L), BF16),
        pltpu.VMEM((2, POINTS, L), F32),
        pltpu.VMEM((3, POINTS, L), F32),
        pltpu.VMEM((2, TOK, L), F32),
        pltpu.VMEM((PARTS, TOK, L), BF16),
        pltpu.VMEM((PARTS, TOK, L), BF16),
        pltpu.VMEM((PARTS, TAPS, L), BF16),
        pltpu.VMEM((2, POINTS, L), F32),
        pltpu.VMEM((PARTS, 3, TOK + 16, L), BF16),
        pltpu.VMEM((PARTS, 3, 16, L), BF16),
        pltpu.VMEM((2 * POINTS, L), BF16),
        pltpu.VMEM((3 * TAPS, L), BF16),
        pltpu.VMEM((2 * TAPS, L), BF16),
        pltpu.VMEM((3, TOK + 16, 128), F32),
        pltpu.VMEM((PARTS, TAPS, L), F32),
        *[pltpu.VMEM(m.shape, BF16) for m in mats],
        pltpu.VMEM((PARTS, TAPS, L), F32),
        pltpu.VMEM((PARTS, GROUP - 1, 8, L), F32),
        pltpu.VMEM((PARTS, 8, L), F32),
        pltpu.VMEM((PARTS, 8, L), F32),
        pltpu.VMEM((PARTS, GROUP, 16, L // 2), BF16),
        pltpu.VMEM((PARTS, TAPS, L), F32),
        pltpu.VMEM((GROUP, 16, 128), F32),
        pltpu.VMEM((PEERS, 16, 128), F32),
        pltpu.VMEM((GROUP, 16, 128), F32),
        dma((PARTS,)),
        dma((len(mats),)),
        dma((PARTS,)),
        dma((PARTS,)),
        dma((3, PARTS)),
        dma((PARTS,)),
        dma((PARTS, 3)),
        dma((PARTS, 3)),
        *[dma((2, PARTS)) for _ in range(7)],
        dma((4,)),
    ]
    d, gl, gs = pl.pallas_call(
        kernel,
        out_shape=(
            jax.ShapeDtypeStruct((3, TOK + 16, CH), BF16),
            jax.ShapeDtypeStruct((TAPS, CH), F32),
            jax.ShapeDtypeStruct((GROUP, 16, 128), F32),
        ),
        in_specs=[anywhere, vmem, anywhere, vmem, anywhere] + [anywhere] * len(mats),
        out_specs=(anywhere, anywhere, vmem),
        scratch_shapes=scratch,
        compiler_params=pltpu.CompilerParams(collective_id=0, has_side_effects=True, vmem_limit_bytes=62 << 20),
        cost_estimate=pl.CostEstimate(flops=20 * 10**9, bytes_accessed=24 * 10**6, transcendentals=0),
    )(projected, short_filters, long_filter, skip_gain[None], cotangent, *mats)
    return finish(short_filters, d, gl, gs)


def solution(mesh):
    placed = (
        P(None, "seq", "ch"),
        P(None, None, "ch"),
        P(None, "ch"),
        P("ch"),
        P(("seq", "ch"), None),
    )
    return jax.shard_map(
        per_device,
        mesh=mesh,
        in_specs=placed,
        out_specs=(P(None, "seq", "ch"), P(None, "ch"), P("ch"), P(None, None, "ch")),
        check_vma=False,
    )
```
